128 devices in a mesh: col: 4 (over y), row: 32 (over z, x, core).
Axes of the slice: x: 4, y: 4, z: 4, core: 2. Of those that a mesh axis runs over, the one named last changes fastest.
Arguments:
- eigenvectors: float32 [256, 131072], P(('col', 'row')), may hold values from -6 to 6
- reflectors: float32 [32, 131072], P('row', 'col'), may hold values from -6 to 6
- sweep_ranges: int32 [32, 2], replicated, may hold values from 0 to 131072, as said below
Outputs:
- transformed: float32 [256, 131072], P('col', 'row')
The draws below stay inside these ranges and needn't reach their ends.
Inputs may be any that keep to these rules, and one draw needn't show every extreme that they name: `sweep_ranges`: in every sweep the first entry is below the second by at least 65536 rows, and sweep 0 covers all 131072 rows.
All inputs are finite; a program needn't handle non-finite values.
Results may differ from the reference program's by a relative error of at most 0.0003.
Values sent between devices are 32-bit elements; how exact they have to be, the bound alone decides.
No kernel may reach another device: no remote copies, remote signals or barrier semaphores. Data moves between devices by JAX's collectives and lax.ppermute only.
A program may use at most 128 MiB of HBM per device.

```python
import jax
import jax.numpy as jnp
from jax import lax

NB = 128
SWEEPS = 32
N = 131072
M = 256


def draw_sweep_ranges(key, part):
    key = jax.random.fold_in(key, 7)
    first_key, second_key = jax.random.split(key)
    lower_rows = jax.random.randint(first_key, (SWEEPS,), 0, N // 4, dtype=jnp.int32)
    upper_rows = N - jax.random.randint(second_key, (SWEEPS,), 0, N // 4, dtype=jnp.int32)
    position = lax.iota(jnp.int32, SWEEPS)
    lower_rows = jnp.where(position == 0, 0, lower_rows)
    upper_rows = jnp.where(position == 0, N, upper_rows)
    return jnp.stack([lower_rows, upper_rows], axis=1).astype(jnp.int32)


def level_of(stream_key, dims, cuts, least, largest):
    gain = 1.0
    for dim, blocks in cuts:
        draws = jax.random.uniform(jax.random.fold_in(jax.random.fold_in(stream_key, 6), dim), (blocks,), jnp.float32, least / len(cuts), largest / len(cuts))
        gain = gain * jnp.repeat(jnp.exp(draws), dims[dim] // blocks).reshape((-1,) + (1,) * (len(dims) - 1 - dim))
    return gain


def centred(stream_key, extent, scale, bound, cuts=(), held_as=jnp.bfloat16):
    result = scale * jax.random.normal(stream_key, extent, jnp.float32)
    if cuts:
        result = result * level_of(stream_key, extent, cuts, -0.22, 0.18)
    return jnp.clip(result, -bound, bound).astype(held_as)


def setup_inputs(seed: int = 0) -> dict:
    keys = jax.random.split(jax.random.key(seed), 4)
    eigenvectors = centred(keys[0], (M, N), 1.0, 6.0, ((0, 128),), jnp.float32)
    reflectors = centred(keys[1], (SWEEPS, N), 1.0, 6.0, ((0, 32), (1, 4)), jnp.float32)
    sweep_ranges = draw_sweep_ranges(jax.random.fold_in(keys[3], 71), 0)
    return {"eigenvectors": eigenvectors, "reflectors": reflectors, "sweep_ranges": sweep_ranges}


def apply_blocks(window, reflector_window, first_start, lower_row, upper_row):
    block_count = reflector_window.shape[0] // NB
    blocks = window.reshape(window.shape[0], block_count, NB)
    vectors = reflector_window.reshape(block_count, NB)
    starts = first_start + NB * lax.iota(jnp.int32, block_count)
    active_mask = jnp.logical_and(starts >= lower_row, starts + NB <= upper_row).astype(jnp.float32)
    squares = jnp.sum(vectors * vectors, axis=1)
    factors = active_mask * 2.0 / (squares + 1.0 - active_mask)
    inner = jnp.einsum("cbi,bi->cb", blocks, vectors, precision=lax.Precision.HIGHEST)
    updated = blocks - (inner * factors[None, :])[:, :, None] * vectors[None, :, :]
    return updated.reshape(window.shape)


def sweep_whole(vectors_in, reflector_row, lower_row, upper_row):
    total_rows = vectors_in.shape[1]
    padded = jnp.pad(vectors_in, ((0, 0), (NB, NB)))
    padded_row = jnp.pad(reflector_row, (NB, NB))
    block_phase = lower_row % NB
    window = lax.dynamic_slice_in_dim(padded, block_phase, total_rows + NB, 1)
    reflector_window = lax.dynamic_slice_in_dim(padded_row, block_phase, total_rows + NB, 0)
    updated = apply_blocks(window, reflector_window, block_phase - NB, lower_row, upper_row)
    padded = lax.dynamic_update_slice_in_dim(padded, updated, block_phase, 1)
    return padded[:, NB:NB + total_rows]


def reference(eigenvectors, reflectors, sweep_ranges):
    def one_sweep(sweep_step, vectors_now):
        sweep_index = SWEEPS - 1 - sweep_step
        reflector_row = lax.dynamic_index_in_dim(reflectors, sweep_index, 0, keepdims=False)
        ranges_now = lax.dynamic_index_in_dim(sweep_ranges, sweep_index, 0, keepdims=False)
        return sweep_whole(vectors_now, reflector_row, ranges_now[0], ranges_now[1])

    return lax.fori_loop(0, SWEEPS, one_sweep, eigenvectors)
```

```python
import jax
import jax.numpy as jnp
from jax import lax
from jax.experimental import pallas as pl
from jax.experimental.pallas import tpu as pltpu
from jax.sharding import PartitionSpec as P

NB = 128
SWEEPS = 32
OWN = 32
EIG = 64
HALO = 32
F32 = jnp.float32
BF16 = jnp.bfloat16
VMEM_LIMIT = 48 * 1024 * 1024


def split(x):
    high = x.astype(BF16)
    low = (x - high.astype(F32)).astype(BF16)
    return high, low


def dot3(left, right, contract):
    lh, ll = split(left)
    rh, rl = split(right)
    dims = (contract, ((), ()))
    def dot(a, b):
        return lax.dot_general(a, b, dims, preferred_element_type=F32)
    return dot(lh, rh) + (dot(lh, rl) + dot(ll, rh))


def lane_group(rows):
    return lax.broadcasted_iota(jnp.int32, (rows, NB), 1) // 32


def sweep_bounds(ranges_ref):
    lower = jnp.broadcast_to(ranges_ref[:, 0:1], (SWEEPS, NB))
    upper = jnp.broadcast_to(ranges_ref[:, 1:2], (SWEEPS, NB))
    phase = lower & (NB - 1)
    first = lower >> 7
    last = (upper - phase - NB) >> 7
    return phase, first, last


def heads_tails(rows, bounds, block):
    phase, first, last = bounds
    lane = lax.broadcasted_iota(jnp.int32, (SWEEPS, NB), 1)
    head_on = (lane >= phase) & (block >= first) & (block <= last)
    tail_on = (lane < phase) & (block - 1 >= first) & (block - 1 <= last)
    return jnp.where(head_on, rows, 0.0), jnp.where(tail_on, rows, 0.0)


def fold(x, rows):
    group = lane_group(rows)
    out = x[0:rows]
    for q in range(1, 4):
        out = jnp.where(group == q, x[q * rows:(q + 1) * rows], out)
    return out


def inner_kernel(base_ref, ranges_ref, x_ref, v_ref, out_ref):
    bounds = sweep_bounds(ranges_ref)
    row = lax.broadcasted_iota(jnp.int32, (SWEEPS, NB), 0)
    lane = lax.broadcasted_iota(jnp.int32, (SWEEPS, NB), 1)
    upper = row <= (lane & 31)
    base = base_ref[0]
    out_ref[0] = jnp.zeros((24, NB), F32)
    for a in range(OWN):
        cols = pl.ds(a * NB, NB)
        head, tail = heads_tails(v_ref[:, cols], bounds, base + a)
        left = jnp.concatenate([x_ref[:, cols], head, tail], axis=0)
        right = jnp.concatenate([head] * 4 + [tail] * 4, axis=0)
        prod = dot3(left, right, ((1,), (1,)))
        from_head, from_tail = prod[:, :NB], prod[:, NB:]
        gram_head = jnp.where(upper, from_head[64:96], from_head[96:128])
        gram_tail = jnp.where(upper, from_tail[96:128], from_tail[64:96])
        out_ref[a + 1, 0:16] = fold(from_head[:64], 16)
        out_ref[a + 1, 16:24] = fold(gram_head, 8)
        out_ref[a, 0:16] += fold(from_tail[:64], 16)
        out_ref[a, 16:24] += fold(gram_tail, 8)


def apply_kernel(base_ref, phase_ref, ranges_ref, own_ref, low_ref, high_ref, x_ref, v_ref,
                 out_ref, gather, coef, tau, inner, shifted, rows_t):
    gather[pl.ds(0, HALO * 24)] = low_ref[pl.ds(24, HALO * 24)]
    gather[pl.ds(HALO * 24, OWN * 24)] = own_ref[pl.ds(24, OWN * 24)]
    gather[pl.ds((HALO - 1) * 24, 24)] += own_ref[pl.ds(0, 24)]
    gather[pl.ds((HALO + OWN - 1) * 24, 24)] += high_ref[pl.ds(0, 24)]
    gather[pl.ds((HALO + OWN) * 24, (HALO - 1) * 24)] = high_ref[pl.ds(24, (HALO - 1) * 24)]
    gather[pl.ds((2 * HALO + OWN - 1) * 24, 33 * 24)] = jnp.zeros((33 * 24, NB), F32)

    for q in range(8):
        block = gather[pl.ds(16 + q, NB, stride=24), :].T
        for g in range(4):
            coef[pl.ds((g * 8 + q) * 32, 32)] = block[g * 32:(g + 1) * 32]
    for j in range(SWEEPS):
        square = coef[pl.ds(j * 33, 1), :]
        tau[pl.ds(j, 1)] = jnp.where(square > 0, 2.0 / jnp.where(square > 0, square, 1.0), 0.0)
    row = lax.broadcasted_iota(jnp.int32, (SWEEPS, NB), 0)
    all_tau = tau[...]
    for j in range(SWEEPS):
        mine = jnp.broadcast_to(all_tau[j:j + 1], (SWEEPS, NB))
        coef[pl.ds(j * 32, 32)] *= jnp.where(row < j, all_tau, mine)

    for q in range(16):
        block = gather[pl.ds(q, NB, stride=24), :].T
        for g in range(4):
            part = block[g * 32:(g + 1) * 32] * all_tau
            inner[pl.ds(g * 16 + q, 32, stride=64), :] = part

    for j in range(SWEEPS - 1, -1, -1):
        total = inner[pl.ds(j * EIG, EIG)]
        for i in range(SWEEPS - 1, j, -1):
            same = coef[pl.ds(j * 32 + i, 1), :]
            next_to = coef[pl.ds(i * 32 + j, 1), :]
            down = jnp.where(phase_ref[j] < phase_ref[i], 0, 1)
            start = pl.multiple_of((2 * i + down) * EIG, EIG)
            total = total - same * inner[pl.ds(i * EIG, EIG)] - next_to * shifted[pl.ds(start, EIG)]
        inner[pl.ds(j * EIG, EIG)] = total
        shifted[pl.ds((2 * j) * EIG, EIG)] = pltpu.roll(total, 1, 1)
        shifted[pl.ds((2 * j + 1) * EIG, EIG)] = pltpu.roll(total, NB - 1, 1)

    for q in range(16):
        parts = [inner[pl.ds(g * 16 + q, 32, stride=64), :] for g in range(4)]
        block = jnp.concatenate(parts, axis=0).T
        rows_t[pl.ds(q, 40, stride=16), :] = block[24:64]

    bounds = sweep_bounds(ranges_ref)
    group = lane_group(16)
    base = base_ref[0]
    for a in range(OWN):
        cols = pl.ds(a * NB, NB)
        head, tail = heads_tails(v_ref[:, cols], bounds, base + a)
        of_head = rows_t[pl.ds((a + 8) * 16, 16)]
        of_tail = rows_t[pl.ds((a + 7) * 16, 16)]
        spread = [jnp.concatenate([jnp.where(group == g, y, 0.0) for g in range(4)], axis=0)
                  for y in (of_head, of_tail)]
        left = jnp.concatenate(spread, axis=1)
        right = jnp.concatenate([head] * 4 + [tail] * 4, axis=0)
        out_ref[:, cols] = x_ref[:, cols] - dot3(left, right, ((1,), (0,)))


def back_transform(x, v, sweep_ranges):
    count = lax.axis_size("row")
    base = (lax.axis_index("row") * OWN).reshape(1).astype(jnp.int32)
    vmem = pl.BlockSpec(memory_space=pltpu.VMEM)
    smem = pl.BlockSpec(memory_space=pltpu.SMEM)
    params = pltpu.CompilerParams(vmem_limit_bytes=VMEM_LIMIT)
    own = pl.pallas_call(
        inner_kernel,
        out_shape=jax.ShapeDtypeStruct((OWN + 1, 24, NB), F32),
        in_specs=[smem, vmem, vmem, vmem],
        out_specs=vmem,
        compiler_params=params,
        name="inner_products",
    )(base, sweep_ranges, x, v)
    own = own.reshape((OWN + 1) * 24, NB)
    forward = [(i, i + 1) for i in range(count - 1)]
    backward = [(i + 1, i) for i in range(count - 1)]
    low = lax.ppermute(own, "row", forward)
    high = lax.ppermute(own, "row", backward)
    phase = sweep_ranges[:, 0] % NB
    return pl.pallas_call(
        apply_kernel,
        out_shape=jax.ShapeDtypeStruct((EIG, OWN * NB), F32),
        in_specs=[smem, smem, vmem, vmem, vmem, vmem, vmem, vmem],
        out_specs=vmem,
        scratch_shapes=[
            pltpu.VMEM((NB * 24, NB), F32),
            pltpu.VMEM((SWEEPS * 32, NB), F32),
            pltpu.VMEM((SWEEPS, NB), F32),
            pltpu.VMEM((SWEEPS * EIG, NB), F32),
            pltpu.VMEM((2 * SWEEPS * EIG, NB), F32),
            pltpu.VMEM((40 * 16, NB), F32),
        ],
        compiler_params=params,
        name="apply_sweeps",
    )(base, phase, sweep_ranges, own, low, high, x, v)


def per_device(eigenvectors, reflectors, sweep_ranges):
    sweep_rows = lax.all_gather(reflectors, "col", axis=1, tiled=True)
    x = lax.all_to_all(eigenvectors, "row", split_axis=1, concat_axis=0, tiled=True)
    v = lax.all_to_all(sweep_rows, "row", split_axis=1, concat_axis=0, tiled=True)
    return back_transform(x, v, sweep_ranges)


def solution(mesh):
    placed = (P(("col", "row"), None), P("row", "col"), P())
    return jax.shard_map(
        per_device, mesh=mesh, in_specs=placed, out_specs=P("col", "row"), check_vma=False
    )
```

```python
import jax
import jax.numpy as jnp
from jax import lax
from jax.experimental import pallas as pl
from jax.experimental.pallas import tpu as pltpu
from jax.sharding import PartitionSpec as P

NB = 128
SWEEPS = 32
OWN = 32
EIG = 64
HALO = 32
F32 = jnp.float32
BF16 = jnp.bfloat16
VMEM_LIMIT = 48 * 1024 * 1024


def split(x):
    high = x.astype(BF16)
    low = (x - high.astype(F32)).astype(BF16)
    return high, low


def dot3(left, right, contract):
    lh, ll = split(left)
    rh, rl = split(right)
    dims = (contract, ((), ()))
    def dot(a, b):
        return lax.dot_general(a, b, dims, preferred_element_type=F32)
    return dot(lh, rh) + (dot(lh, rl) + dot(ll, rh))


def lane_group(rows):
    return lax.broadcasted_iota(jnp.int32, (rows, NB), 1) // 32


def sweep_bounds(ranges_ref):
    lower = jnp.broadcast_to(ranges_ref[:, 0:1], (SWEEPS, NB))
    upper = jnp.broadcast_to(ranges_ref[:, 1:2], (SWEEPS, NB))
    phase = lower & (NB - 1)
    first = lower >> 7
    last = (upper - phase - NB) >> 7
    return phase, first, last


def heads_tails(rows, bounds, block):
    phase, first, last = bounds
    lane = lax.broadcasted_iota(jnp.int32, (SWEEPS, NB), 1)
    head_on = (lane >= phase) & (block >= first) & (block <= last)
    tail_on = (lane < phase) & (block - 1 >= first) & (block - 1 <= last)
    return jnp.where(head_on, rows, 0.0), jnp.where(tail_on, rows, 0.0)


def fold(x, rows):
    group = lane_group(rows)
    out = x[0:rows]
    for q in range(1, 4):
        out = jnp.where(group == q, x[q * rows:(q + 1) * rows], out)
    return out


def inner_kernel(place_ref, ranges_ref, x_ref, v0, v1, v2, v3, out_ref, v_ref):
    for k, piece in enumerate((v0, v1, v2, v3)):
        first = pl.multiple_of(((place_ref[1] + k) & 3) * 8, 8)
        v_ref[pl.ds(first, 8), :] = piece[...]
    bounds = sweep_bounds(ranges_ref)
    row = lax.broadcasted_iota(jnp.int32, (SWEEPS, NB), 0)
    lane = lax.broadcasted_iota(jnp.int32, (SWEEPS, NB), 1)
    upper = row <= (lane & 31)
    base = place_ref[0] * OWN
    out_ref[0] = jnp.zeros((24, NB), F32)
    for a in range(OWN):
        cols = pl.ds(a * NB, NB)
        head, tail = heads_tails(v_ref[:, cols], bounds, base + a)
        left = jnp.concatenate([x_ref[:, cols], head, tail], axis=0)
        right = jnp.concatenate([head] * 4 + [tail] * 4, axis=0)
        prod = dot3(left, right, ((1,), (1,)))
        from_head, from_tail = prod[:, :NB], prod[:, NB:]
        gram_head = jnp.where(upper, from_head[64:96], from_head[96:128])
        gram_tail = jnp.where(upper, from_tail[96:128], from_tail[64:96])
        out_ref[a + 1, 0:16] = fold(from_head[:64], 16)
        out_ref[a + 1, 16:24] = fold(gram_head, 8)
        out_ref[a, 0:16] += fold(from_tail[:64], 16)
        out_ref[a, 16:24] += fold(gram_tail, 8)


def apply_kernel(place_ref, phase_ref, ranges_ref, own_ref, pair_ref, other_ref, x_ref, v_ref,
                 out_ref, gather, coef, tau, inner, shifted, rows_t):
    gather[pl.ds(HALO * 24, OWN * 24)] = own_ref[pl.ds(24, OWN * 24)]
    gather[pl.ds((HALO - 1) * 24, 24)] = own_ref[pl.ds(0, 24)]

    def take(low_ref, high_ref):
        gather[pl.ds(0, (HALO - 1) * 24)] = low_ref[pl.ds(24, (HALO - 1) * 24)]
        gather[pl.ds((HALO - 1) * 24, 24)] += low_ref[pl.ds(HALO * 24, 24)]
        gather[pl.ds((HALO + OWN - 1) * 24, 24)] += high_ref[pl.ds(0, 24)]
        gather[pl.ds((HALO + OWN) * 24, (HALO - 1) * 24)] = high_ref[pl.ds(24, (HALO - 1) * 24)]

    odd = place_ref[0] & 1

    @pl.when(odd == 0)
    def _():
        take(other_ref, pair_ref)

    @pl.when(odd == 1)
    def _():
        take(pair_ref, other_ref)

    gather[pl.ds((2 * HALO + OWN - 1) * 24, 33 * 24)] = jnp.zeros((33 * 24, NB), F32)

    for q in range(8):
        block = gather[pl.ds(16 + q, NB, stride=24), :].T
        for g in range(4):
            coef[pl.ds((g * 8 + q) * 32, 32)] = block[g * 32:(g + 1) * 32]
    for j in range(SWEEPS):
        square = coef[pl.ds(j * 33, 1), :]
        tau[pl.ds(j, 1)] = jnp.where(square > 0, 2.0 / jnp.where(square > 0, square, 1.0), 0.0)
    row = lax.broadcasted_iota(jnp.int32, (SWEEPS, NB), 0)
    all_tau = tau[...]
    for j in range(SWEEPS):
        mine = jnp.broadcast_to(all_tau[j:j + 1], (SWEEPS, NB))
        coef[pl.ds(j * 32, 32)] *= jnp.where(row < j, all_tau, mine)

    for q in range(16):
        block = gather[pl.ds(q, NB, stride=24), :].T
        for g in range(4):
            part = block[g * 32:(g + 1) * 32] * all_tau
            inner[pl.ds(g * 16 + q, 32, stride=64), :] = part

    for j in range(SWEEPS - 1, -1, -1):
        total = inner[pl.ds(j * EIG, EIG)]
        for i in range(SWEEPS - 1, j, -1):
            same = coef[pl.ds(j * 32 + i, 1), :]
            next_to = coef[pl.ds(i * 32 + j, 1), :]
            down = jnp.where(phase_ref[j] < phase_ref[i], 0, 1)
            start = pl.multiple_of((2 * i + down) * EIG, EIG)
            total = total - same * inner[pl.ds(i * EIG, EIG)] - next_to * shifted[pl.ds(start, EIG)]
        inner[pl.ds(j * EIG, EIG)] = total
        shifted[pl.ds((2 * j) * EIG, EIG)] = pltpu.roll(total, 1, 1)
        shifted[pl.ds((2 * j + 1) * EIG, EIG)] = pltpu.roll(total, NB - 1, 1)

    for q in range(16):
        parts = [inner[pl.ds(g * 16 + q, 32, stride=64), :] for g in range(4)]
        block = jnp.concatenate(parts, axis=0).T
        rows_t[pl.ds(q, 40, stride=16), :] = block[24:64]

    bounds = sweep_bounds(ranges_ref)
    group = lane_group(16)
    base = place_ref[0] * OWN
    for a in range(OWN):
        cols = pl.ds(a * NB, NB)
        head, tail = heads_tails(v_ref[:, cols], bounds, base + a)
        of_head = rows_t[pl.ds((a + 8) * 16, 16)]
        of_tail = rows_t[pl.ds((a + 7) * 16, 16)]
        spread = [jnp.concatenate([jnp.where(group == g, y, 0.0) for g in range(4)], axis=0)
                  for y in (of_head, of_tail)]
        left = jnp.concatenate(spread, axis=1)
        right = jnp.concatenate([head] * 4 + [tail] * 4, axis=0)
        out_ref[:, cols] = x_ref[:, cols] - dot3(left, right, ((1,), (0,)))


def back_transform(x, pieces, sweep_ranges):
    count = lax.axis_size("row")
    place = jnp.stack([lax.axis_index("row"), lax.axis_index("col")]).astype(jnp.int32)
    vmem = pl.BlockSpec(memory_space=pltpu.VMEM)
    smem = pl.BlockSpec(memory_space=pltpu.SMEM)
    params = pltpu.CompilerParams(vmem_limit_bytes=VMEM_LIMIT)
    own, v = pl.pallas_call(
        inner_kernel,
        out_shape=(
            jax.ShapeDtypeStruct((OWN + 1, 24, NB), F32),
            jax.ShapeDtypeStruct((SWEEPS, OWN * NB), F32),
        ),
        in_specs=[smem, vmem] + [vmem] * 5,
        out_specs=(vmem, vmem),
        compiler_params=params,
        name="inner_products",
    )(place, sweep_ranges, x, *pieces)
    own = own.reshape((OWN + 1) * 24, NB)
    within = [(i, i ^ 1) for i in range(count)]
    across = [(i, i + 1) for i in range(1, count - 1, 2)]
    across = across + [(t, s) for s, t in across]
    pair = lax.ppermute(own, "row", within)
    other = lax.ppermute(own, "row", across)
    phase = sweep_ranges[:, 0] % NB
    return pl.pallas_call(
        apply_kernel,
        out_shape=jax.ShapeDtypeStruct((EIG, OWN * NB), F32),
        in_specs=[smem, smem, vmem, vmem, vmem, vmem, vmem, vmem],
        out_specs=vmem,
        scratch_shapes=[
            pltpu.VMEM((NB * 24, NB), F32),
            pltpu.VMEM((SWEEPS * 32, NB), F32),
            pltpu.VMEM((SWEEPS, NB), F32),
            pltpu.VMEM((SWEEPS * EIG, NB), F32),
            pltpu.VMEM((2 * SWEEPS * EIG, NB), F32),
            pltpu.VMEM((40 * 16, NB), F32),
        ],
        compiler_params=params,
        name="apply_sweeps",
    )(place, phase, sweep_ranges, own, pair, other, x, v)


def sweep_pieces(reflectors):
    cols, count = lax.axis_size("col"), lax.axis_size("row")
    width = count // cols
    groups = [[g * width + q for q in range(width)] for g in range(cols)]
    mine = lax.all_to_all(
        reflectors.reshape(width, -1), "row", split_axis=0, concat_axis=0, tiled=True,
        axis_index_groups=groups,
    )
    pieces = []
    for k in range(cols):
        pairs = [
            (c * count + g * width + q, ((g - k) % cols) * count + c * width + q)
            for c in range(cols) for g in range(cols) for q in range(width)
        ]
        pieces.append(lax.ppermute(mine, ("col", "row"), pairs))
    return pieces


def per_device(eigenvectors, reflectors, sweep_ranges):
    pieces = sweep_pieces(reflectors)
    x = lax.all_to_all(eigenvectors, "row", split_axis=1, concat_axis=0, tiled=True)
    return back_transform(x, pieces, sweep_ranges)


def solution(mesh):
    placed = (P(("col", "row"), None), P("row", "col"), P())
    return jax.shard_map(
        per_device, mesh=mesh, in_specs=placed, out_specs=P("col", "row"), check_vma=False
    )
```

```python
import jax
import jax.numpy as jnp
from jax import lax
from jax.experimental import pallas as pl
from jax.experimental.pallas import tpu as pltpu
from jax.sharding import PartitionSpec as P

NB = 128
SWEEPS = 32
OWN = 32
EIG = 64
HALO = 32
ROWS = 24
F32 = jnp.float32
BF16 = jnp.bfloat16
VMEM_LIMIT = 48 * 1024 * 1024


def split(x):
    high = x.astype(BF16)
    low = (x - high.astype(F32)).astype(BF16)
    return high, low


def lane_group(rows):
    return lax.broadcasted_iota(jnp.int32, (rows, NB), 1) // 32


def sweep_bounds(ranges_ref):
    lower = jnp.broadcast_to(ranges_ref[:, 0:1], (SWEEPS, NB))
    upper = jnp.broadcast_to(ranges_ref[:, 1:2], (SWEEPS, NB))
    phase = lower & (NB - 1)
    first = lower >> 7
    last = (upper - phase - NB) >> 7
    return phase, first, last


def heads_tails(rows, bounds, block):
    phase, first, last = bounds
    lane = lax.broadcasted_iota(jnp.int32, (SWEEPS, NB), 1)
    head_on = (lane >= phase) & (block >= first) & (block <= last)
    tail_on = (lane < phase) & (block - 1 >= first) & (block - 1 <= last)
    return jnp.where(head_on, rows, 0.0), jnp.where(tail_on, rows, 0.0)


def fold(x, rows):
    group = lane_group(rows)
    turned = pltpu.roll(x, 32, 1)
    def keep(even, odd):
        parts = [(even if q % 2 == 0 else odd)[q * rows:(q + 1) * rows] for q in range(4)]
        out = parts[0]
        for q in range(1, 4):
            out = jnp.where(group == q, parts[q], out)
        return out
    return keep(x, turned), keep(turned, x)


def inner_products(x, right_high, right_low):
    left = jnp.concatenate(split(x), axis=1)
    right = jnp.concatenate([right_high] * 2 + [right_low] * 2, axis=0)
    right = jnp.concatenate([right, right], axis=1)
    prod = lax.dot_general(left, right, (((1,), (1,)), ((), ())), preferred_element_type=F32)
    return prod[:, :NB] + prod[:, NB:]


def outer_products(y, right_high, right_low):
    left = jnp.concatenate(split(y), axis=0)
    def four(both):
        return jnp.concatenate([both[:32]] * 4 + [both[32:]] * 4, axis=0)
    right = jnp.concatenate([four(right_high), four(right_low)], axis=1)
    prod = lax.dot_general(left, right, (((1,), (0,)), ((), ())), preferred_element_type=F32)
    prod = prod[:64] + prod[64:]
    return prod[:, :NB] + prod[:, NB:]


def needed(k):
    lane = lax.broadcasted_iota(jnp.int32, (ROWS, NB), 1) & 31
    return lane >= k - 1


def pack(ref, row_of, message):
    def block(k):
        return ref[pl.ds(row_of(k) * ROWS, ROWS)]

    message[pl.ds(0, ROWS)] = block(1)
    for k in range(2, 17):
        other = pltpu.roll(block(34 - k), NB - 33 + k, 1)
        message[pl.ds((k - 1) * ROWS, ROWS)] = jnp.where(needed(k), block(k), other)
    message[pl.ds(16 * ROWS, ROWS)] = block(17)


def unpack(message, valid=None):
    def block(m):
        data = message[pl.ds(m * ROWS, ROWS)]
        return data if valid is None else jnp.where(valid, data, 0.0)

    yield 1, block(0)
    for k in range(2, 17):
        both = block(k - 1)
        yield k, jnp.where(needed(k), both, 0.0)
        yield 34 - k, jnp.where(needed(34 - k), pltpu.roll(both, 33 - k, 1), 0.0)
    yield 17, jnp.where(needed(17), block(16), 0.0)


def inner_kernel(place_ref, ranges_ref, arrived_ref, v0, v1, v2, v3,
                 out_ref, pair_ref, other_ref, high_ref, low_ref, x_ref, v_ref):
    for k, piece in enumerate((v0, v1, v2, v3)):
        first = pl.multiple_of(((place_ref[1] + k) & 3) * 8, 8)
        v_ref[pl.ds(first, 8), :] = piece[...]
    bounds = sweep_bounds(ranges_ref)
    row = lax.broadcasted_iota(jnp.int32, (SWEEPS, NB), 0)
    lane = lax.broadcasted_iota(jnp.int32, (SWEEPS, NB), 1)
    upper = row <= (lane & 31)
    heads = (lane & 32) == 0
    base = place_ref[0] * OWN
    out_ref[pl.ds(0, ROWS)] = jnp.zeros((ROWS, NB), F32)
    for a in range(OWN):
        cols = pl.ds(a * NB, NB)
        head, tail = heads_tails(v_ref[:, cols], bounds, base + a)
        high, low = split(jnp.concatenate([head, tail], axis=0))
        high_ref[pl.ds(a * 64, 64)] = high
        low_ref[pl.ds(a * 64, 64)] = low
        x = arrived_ref[:, :, cols].reshape(EIG, NB)
        x_ref[:, cols] = x
        inner = inner_products(jnp.concatenate([x, head, tail], axis=0), high, low)
        of_head, of_tail = inner[64:96], inner[96:128]
        gram = jnp.where(upper == heads, of_head, of_tail)
        inner_head, inner_tail = fold(inner[:64], 16)
        gram_head, gram_tail = fold(gram, 8)
        out_ref[pl.ds((a + 1) * ROWS, 16)] = inner_head
        out_ref[pl.ds((a + 1) * ROWS + 16, 8)] = gram_head
        out_ref[pl.ds(a * ROWS, 16)] += inner_tail
        out_ref[pl.ds(a * ROWS + 16, 8)] += gram_tail

    def to_next(message):
        pack(out_ref, lambda k: 33 - k, message)

    def to_last(message):
        pack(out_ref, lambda k: k - 1, message)

    odd = place_ref[0] & 1

    @pl.when(odd == 0)
    def _():
        to_next(pair_ref)
        to_last(other_ref)

    @pl.when(odd == 1)
    def _():
        to_last(pair_ref)
        to_next(other_ref)


def apply_kernel(place_ref, phase_ref, own_ref, pair_ref, other_ref, x_ref, high_ref, low_ref,
                 out_ref, gather, coef, inner, rows_t, *shifted):
    def at(place, count=1):
        return pl.ds(place * ROWS, count * ROWS)

    gather[at(HALO, OWN)] = own_ref[at(1, OWN)]
    gather[at(2 * HALO + OWN - 1, 33)] = jnp.zeros((33 * ROWS, NB), F32)
    gather[at(HALO - 1)] = own_ref[at(0)]

    def take(low_blocks, high_blocks):
        for k, block in low_blocks:
            if k == 1:
                gather[at(HALO - 1)] += block
            else:
                gather[at(HALO - k)] = block
        for k, block in high_blocks:
            if k == 1:
                gather[at(HALO + OWN - 1)] += block
            else:
                gather[at(HALO + OWN - 2 + k)] = block

    odd = place_ref[0] & 1

    @pl.when(odd == 0)
    def _():
        take(unpack(other_ref, place_ref[0] > 0), unpack(pair_ref))

    @pl.when(odd == 1)
    def _():
        take(unpack(pair_ref), unpack(other_ref, place_ref[0] < place_ref[2] - 1))

    for q in range(8):
        block = gather[pl.ds(16 + q, NB, stride=ROWS), :].T
        for g in range(4):
            coef[pl.ds((g * 8 + q) * 32, 32)] = block[g * 32:(g + 1) * 32]
    square = coef[pl.ds(0, SWEEPS, stride=33), :]
    all_tau = jnp.where(square > 0, 2.0 / jnp.where(square > 0, square, 1.0), 0.0)
    row = lax.broadcasted_iota(jnp.int32, (SWEEPS, NB), 0)
    for j in range(SWEEPS):
        mine = jnp.broadcast_to(all_tau[j:j + 1], (SWEEPS, NB))
        coef[pl.ds(j * 32, 32)] *= jnp.where(row < j, all_tau, mine)

    for q in range(16):
        block = gather[pl.ds(q, NB, stride=ROWS), :].T
        for g in range(4):
            part = block[g * 32:(g + 1) * 32] * all_tau
            inner[pl.ds(g * 16 + q, 32, stride=64), :] = part

    phases = [phase_ref[j] for j in range(SWEEPS)]
    for j in range(SWEEPS - 1, -1, -1):
        total = inner[pl.ds(j * EIG, EIG)]
        for i in range(SWEEPS - 1, j, -1):
            same = coef[pl.ds(j * 32 + i, 1), :]
            next_to = coef[pl.ds(i * 32 + j, 1), :]
            start = pl.multiple_of(jnp.where(phases[j] < phases[i], 0, EIG), EIG)
            total = total - same * inner[pl.ds(i * EIG, EIG)] - next_to * shifted[i][pl.ds(start, EIG)]
        inner[pl.ds(j * EIG, EIG)] = total
        if j > 0:
            shifted[j][pl.ds(0, EIG)] = pltpu.roll(total, 1, 1)
            shifted[j][pl.ds(EIG, EIG)] = pltpu.roll(total, NB - 1, 1)

    for q in range(16):
        parts = [inner[pl.ds(g * 16 + q, 32, stride=64), :] for g in range(4)]
        block = jnp.concatenate(parts, axis=0).T
        rows_t[pl.ds(q, 40, stride=16), :] = block[24:64]

    group = lane_group(16)
    for a in range(OWN):
        cols = pl.ds(a * NB, NB)
        rows = pl.ds(a * 64, 64)
        of_head = rows_t[pl.ds((a + 8) * 16, 16)]
        of_tail = rows_t[pl.ds((a + 7) * 16, 16)]
        spread = [jnp.concatenate([jnp.where(group == g, y, 0.0) for g in range(4)], axis=0)
                  for y in (of_head, of_tail)]
        update = outer_products(jnp.concatenate(spread, axis=1), high_ref[rows], low_ref[rows])
        out_ref[:, cols] = x_ref[:, cols] - update


def call(kernel, name, out_shape, scratch, operands):
    vmem = pl.BlockSpec(memory_space=pltpu.VMEM)
    smem = pl.BlockSpec(memory_space=pltpu.SMEM)
    specs = [smem if x.ndim == 1 else vmem for x in operands]
    return pl.pallas_call(
        kernel,
        out_shape=tuple(jax.ShapeDtypeStruct(*x) for x in out_shape),
        in_specs=specs,
        out_specs=(vmem,) * len(out_shape),
        scratch_shapes=[pltpu.VMEM(x, F32) for x in scratch],
        compiler_params=pltpu.CompilerParams(vmem_limit_bytes=VMEM_LIMIT),
        name=name,
    )(*operands)


def back_transform(x, pieces, sweep_ranges):
    count = lax.axis_size("row")
    place = jnp.stack([lax.axis_index("row"), lax.axis_index("col"), count]).astype(jnp.int32)
    phase = sweep_ranges[:, 0] % NB
    message = ((17 * ROWS, NB), F32)
    own, to_pair, to_other, high, low, x = call(
        inner_kernel, "inner_products",
        [(((OWN + 1) * ROWS, NB), F32), message, message, ((OWN * 64, NB), BF16), ((OWN * 64, NB), BF16), ((EIG, OWN * NB), F32)],
        [(SWEEPS, OWN * NB)],
        [place, sweep_ranges, x, *pieces],
    )
    within = [(i, i ^ 1) for i in range(count)]
    across = [(i, (i + 1) % count) for i in range(1, count, 2)]
    across = across + [(t, s) for s, t in across]
    pair = lax.ppermute(to_pair, "row", within)
    other = lax.ppermute(to_other, "row", across)
    out, = call(
        apply_kernel, "apply_sweeps",
        [((EIG, OWN * NB), F32)],
        [(NB * ROWS, NB), (SWEEPS * 32, NB), (SWEEPS * EIG, NB), (40 * 16, NB)] + [(2 * EIG, NB)] * SWEEPS,
        [place, phase, own, pair, other, x, high, low],
    )
    return out


def sweep_pieces(reflectors):
    cols, count = lax.axis_size("col"), lax.axis_size("row")
    width = count // cols
    groups = [[g * width + q for q in range(width)] for g in range(cols)]
    mine = lax.all_to_all(
        reflectors.reshape(width, -1), "row", split_axis=0, concat_axis=0, tiled=True,
        axis_index_groups=groups,
    )
    pieces = []
    for k in range(cols):
        pairs = [
            (c * count + g * width + q, ((g - k) % cols) * count + c * width + q)
            for c in range(cols) for g in range(cols) for q in range(width)
        ]
        pieces.append(lax.ppermute(mine, ("col", "row"), pairs))
    return pieces


def per_device(eigenvectors, reflectors, sweep_ranges):
    pieces = sweep_pieces(reflectors)
    x = lax.all_to_all(eigenvectors.reshape(2, -1, OWN * NB), "row", split_axis=1, concat_axis=1, tiled=True)
    x = x.transpose(1, 0, 2)
    return back_transform(x, pieces, sweep_ranges)


def solution(mesh):
    placed = (P(("col", "row"), None), P("row", "col"), P())
    return jax.shard_map(
        per_device, mesh=mesh, in_specs=placed, out_specs=P("col", "row"), check_vma=False
    )
```

```python
import jax
import jax.numpy as jnp
from jax import lax
from jax.experimental import pallas as pl
from jax.experimental.pallas import tpu as pltpu
from jax.sharding import PartitionSpec as P

NB = 128
SWEEPS = 32
OWN = 32
EIG = 64
HALO = 32
PART = 8
WIDE = 16
ROWS = 24
F32 = jnp.float32
BF16 = jnp.bfloat16
VMEM_LIMIT = 48 * 1024 * 1024


def split(x):
    high = x.astype(BF16)
    low = (x - high.astype(F32)).astype(BF16)
    return high, low


def halves(low, high):
    lane = lax.broadcasted_iota(jnp.int32, low.shape, 1)
    return jnp.where(lane < 64, pltpu.roll(low, NB - 16, 1), pltpu.roll(high, 48, 1))


def lane_group(rows):
    return lax.broadcasted_iota(jnp.int32, (rows, NB), 1) // 32


def sweep_bounds(ranges_ref):
    lower = jnp.broadcast_to(ranges_ref[:, 0:1], (SWEEPS, NB))
    upper = jnp.broadcast_to(ranges_ref[:, 1:2], (SWEEPS, NB))
    phase = lower & (NB - 1)
    first = lower >> 7
    last = (upper - phase - NB) >> 7
    return phase, first, last


def heads_tails(rows, bounds, block):
    phase, first, last = bounds
    lane = lax.broadcasted_iota(jnp.int32, (SWEEPS, NB), 1)
    head_on = (lane >= phase) & (block >= first) & (block <= last)
    tail_on = (lane < phase) & (block - 1 >= first) & (block - 1 <= last)
    return jnp.where(head_on, rows, 0.0), jnp.where(tail_on, rows, 0.0)


def fold(x, rows):
    group = lane_group(rows)
    turned = pltpu.roll(x, 32, 1)
    def keep(even, odd):
        parts = [(even if q % 2 == 0 else odd)[q * rows:(q + 1) * rows] for q in range(4)]
        out = parts[0]
        for q in range(1, 4):
            out = jnp.where(group == q, parts[q], out)
        return out
    return keep(x, turned), keep(turned, x)


def inner_products(x, right_high, right_low):
    left = jnp.concatenate(split(x), axis=1)
    right = jnp.concatenate([right_high] * 2 + [right_low] * 2, axis=0)
    right = jnp.concatenate([right, right], axis=1)
    prod = lax.dot_general(left, right, (((1,), (1,)), ((), ())), preferred_element_type=F32)
    return prod[:, :NB] + prod[:, NB:]


def outer_products(y, right_high, right_low):
    left = jnp.concatenate(split(y), axis=0)
    def four(both):
        return jnp.concatenate([both[:32]] * 4 + [both[32:]] * 4, axis=0)
    right = jnp.concatenate([four(right_high), four(right_low)], axis=1)
    prod = lax.dot_general(left, right, (((1,), (0,)), ((), ())), preferred_element_type=F32)
    prod = prod[:64] + prod[64:]
    return prod[:, :NB] + prod[:, NB:]


def needed(k):
    lane = lax.broadcasted_iota(jnp.int32, (ROWS, NB), 1) & 31
    return lane >= k - 1


def pack(ref, row_of, message):
    def block(k):
        return ref[pl.ds(row_of(k) * ROWS, ROWS)]

    message[pl.ds(0, ROWS)] = block(1)
    for k in range(2, 17):
        other = pltpu.roll(block(34 - k), NB - 33 + k, 1)
        message[pl.ds((k - 1) * ROWS, ROWS)] = jnp.where(needed(k), block(k), other)
    message[pl.ds(16 * ROWS, ROWS)] = block(17)


def unpack(message, valid=None):
    def block(m):
        data = message[pl.ds(m * ROWS, ROWS)]
        return data if valid is None else jnp.where(valid, data, 0.0)

    yield 1, block(0)
    for k in range(2, 17):
        both = block(k - 1)
        yield k, jnp.where(needed(k), both, 0.0)
        yield 34 - k, jnp.where(needed(34 - k), pltpu.roll(both, 33 - k, 1), 0.0)
    yield 17, jnp.where(needed(17), block(16), 0.0)


def inner_kernel(place_ref, ranges_ref, arrived_ref, v0, v1, v2, v3,
                 out_ref, pair_ref, other_ref, high_ref, low_ref, x_ref, v_ref):
    for k, piece in enumerate((v0, v1, v2, v3)):
        first = pl.multiple_of(((place_ref[1] + k) & 3) * 8, 8)
        v_ref[pl.ds(first, 8), :] = piece[...]
    bounds = sweep_bounds(ranges_ref)
    row = lax.broadcasted_iota(jnp.int32, (SWEEPS, NB), 0)
    lane = lax.broadcasted_iota(jnp.int32, (SWEEPS, NB), 1)
    upper = row <= (lane & 31)
    heads = (lane & 32) == 0
    base = place_ref[0] * OWN
    out_ref[pl.ds(0, ROWS)] = jnp.zeros((ROWS, NB), F32)
    for a in range(OWN):
        cols = pl.ds(a * NB, NB)
        head, tail = heads_tails(v_ref[:, cols], bounds, base + a)
        high, low = split(jnp.concatenate([head, tail], axis=0))
        high_ref[pl.ds(a * 64, 64)] = high
        low_ref[pl.ds(a * 64, 64)] = low
        x = arrived_ref[:, :, cols].reshape(EIG, NB)
        x_ref[:, cols] = x
        inner = inner_products(jnp.concatenate([x, head, tail], axis=0), high, low)
        of_head, of_tail = inner[64:96], inner[96:128]
        gram = jnp.where(upper == heads, of_head, of_tail)
        inner_head, inner_tail = fold(inner[:64], 16)
        gram_head, gram_tail = fold(gram, 8)
        out_ref[pl.ds((a + 1) * ROWS, 16)] = inner_head
        out_ref[pl.ds((a + 1) * ROWS + 16, 8)] = gram_head
        out_ref[pl.ds(a * ROWS, 16)] += inner_tail
        out_ref[pl.ds(a * ROWS + 16, 8)] += gram_tail

    def to_next(message):
        pack(out_ref, lambda k: 33 - k, message)

    def to_last(message):
        pack(out_ref, lambda k: k - 1, message)

    odd = place_ref[0] & 1

    @pl.when(odd == 0)
    def _():
        to_next(pair_ref)
        to_last(other_ref)

    @pl.when(odd == 1)
    def _():
        to_last(pair_ref)
        to_next(other_ref)


def apply_kernel(place_ref, phase_ref, own_ref, pair_ref, other_ref, x_ref, high_ref, low_ref,
                 out_ref, result, sems, gather, coef, coef_half, inner, inner_half, rows_t, *shifted):
    def at(place, count=1):
        return pl.ds(place * ROWS, count * ROWS)

    gather[at(HALO, OWN)] = own_ref[at(1, OWN)]
    gather[at(2 * HALO + OWN - 1, 33)] = jnp.zeros((33 * ROWS, NB), F32)
    gather[at(HALO - 1)] = own_ref[at(0)]

    def take(low_blocks, high_blocks):
        for k, block in low_blocks:
            if k == 1:
                gather[at(HALO - 1)] += block
            else:
                gather[at(HALO - k)] = block
        for k, block in high_blocks:
            if k == 1:
                gather[at(HALO + OWN - 1)] += block
            else:
                gather[at(HALO + OWN - 2 + k)] = block

    odd = place_ref[0] & 1

    @pl.when(odd == 0)
    def _():
        take(unpack(other_ref, place_ref[0] > 0), unpack(pair_ref))

    @pl.when(odd == 1)
    def _():
        take(unpack(pair_ref), unpack(other_ref, place_ref[0] < place_ref[2] - 1))

    for q in range(8):
        block = gather[pl.ds(16 + q, NB, stride=ROWS), :].T
        for g in range(4):
            coef[pl.ds((g * 8 + q) * 32, 32)] = block[g * 32:(g + 1) * 32]
    square = coef[pl.ds(0, SWEEPS, stride=33), :]
    all_tau = jnp.where(square > 0, 2.0 / jnp.where(square > 0, square, 1.0), 0.0)
    row = lax.broadcasted_iota(jnp.int32, (SWEEPS, NB), 0)
    for j in range(SWEEPS):
        mine = jnp.broadcast_to(all_tau[j:j + 1], (SWEEPS, NB))
        scaled = coef[pl.ds(j * 32, 32)] * jnp.where(row < j, all_tau, mine)
        coef[pl.ds(j * 32, 32)] = scaled
        count = 32 if j < WIDE else 16
        coef_half[pl.ds(j * 32, count)] = halves(scaled[:count], scaled[:count])

    for q in range(16):
        block = gather[pl.ds(q, NB, stride=ROWS), :].T
        parts = [block[g * 32:(g + 1) * 32] * all_tau for g in range(4)]
        for g in range(4):
            inner[pl.ds(g * 16 + q + 8 * EIG, 24, stride=64), :] = parts[g][8:]
        for g in range(2):
            inner_half[pl.ds(g * 16 + q, 16, stride=32), :] = halves(parts[g][:16], parts[g + 2][:16])

    phases = [phase_ref[j] for j in range(SWEEPS)]
    wide, half = shifted[:SWEEPS - WIDE], shifted[SWEEPS - WIDE:]
    lane = lax.broadcasted_iota(jnp.int32, (EIG // 2, NB), 1) & 63

    def keep_half(j, y):
        half[j][pl.ds(0, 32)] = jnp.where(lane == 0, 0.0, pltpu.roll(y, 1, 1))
        half[j][pl.ds(32, 32)] = jnp.where(lane == 63, 0.0, pltpu.roll(y, NB - 1, 1))

    for j in range(SWEEPS - 1, WIDE - 2, -1):
        total = inner[pl.ds(j * EIG, EIG)]
        for i in range(SWEEPS - 1, j, -1):
            same = coef[pl.ds(j * 32 + i, 1), :]
            next_to = coef[pl.ds(i * 32 + j, 1), :]
            start = pl.multiple_of(jnp.where(phases[j] < phases[i], 0, EIG), EIG)
            total = total - same * inner[pl.ds(i * EIG, EIG)] - next_to * wide[i - WIDE][pl.ds(start, EIG)]
        inner[pl.ds(j * EIG, EIG)] = total
        if j >= WIDE:
            wide[j - WIDE][pl.ds(0, EIG)] = pltpu.roll(total, 1, 1)
            wide[j - WIDE][pl.ds(EIG, EIG)] = pltpu.roll(total, NB - 1, 1)
        both = halves(total[:32], total[32:])
        inner_half[pl.ds(j * 32, 32)] = both
        keep_half(j, both)

    for j in range(WIDE - 2, -1, -1):
        total = inner_half[pl.ds(j * 32, 32)]
        for i in range(SWEEPS - 1, j, -1):
            same = coef_half[pl.ds(j * 32 + i, 1), :]
            next_to = coef_half[pl.ds(i * 32 + j, 1), :]
            start = pl.multiple_of(jnp.where(phases[j] < phases[i], 0, 32), 32)
            total = total - same * inner_half[pl.ds(i * 32, 32)] - next_to * half[i][pl.ds(start, 32)]
        inner_half[pl.ds(j * 32, 32)] = total
        if j > 0:
            keep_half(j, total)

    for t in range(8):
        parts = [inner_half[pl.ds(g * 16 + q * 8 + t, 32, stride=32), :] for q in range(2) for g in range(2)]
        block = jnp.concatenate(parts, axis=0).T
        for h in range(2):
            rows_t[pl.ds(h * 8 + t, 40, stride=16), :] = block[h * 64 + 8:h * 64 + 48]

    def copy_out(c):
        part = pl.ds(c * PART * NB, PART * NB)
        return pltpu.make_async_copy(result.at[:, part], out_ref.at[:, part], sems.at[c])

    group = lane_group(8)
    for a in range(OWN):
        cols = pl.ds(a * NB, NB)
        rows = pl.ds(a * 64, 64)
        of_head = rows_t[pl.ds((a + 8) * 16, 16)]
        of_tail = rows_t[pl.ds((a + 7) * 16, 16)]
        spread = [jnp.concatenate([jnp.where(group == q * 2 + g, y[h * 8:h * 8 + 8], 0.0)
                                   for h in range(2) for g in range(2) for q in range(2)], axis=0)
                  for y in (of_head, of_tail)]
        update = outer_products(jnp.concatenate(spread, axis=1), high_ref[rows], low_ref[rows])
        result[:, cols] = x_ref[:, cols] - update
        if (a + 1) % PART == 0:
            copy_out(a // PART).start()
    for c in range(OWN // PART):
        copy_out(c).wait()


def call(kernel, name, out_shape, scratch, operands, space=pltpu.VMEM):
    vmem = pl.BlockSpec(memory_space=pltpu.VMEM)
    smem = pl.BlockSpec(memory_space=pltpu.SMEM)
    specs = [smem if x.ndim == 1 else vmem for x in operands]
    return pl.pallas_call(
        kernel,
        out_shape=tuple(jax.ShapeDtypeStruct(*x) for x in out_shape),
        in_specs=specs,
        out_specs=(pl.BlockSpec(memory_space=space),) * len(out_shape),
        scratch_shapes=[pltpu.VMEM(x, F32) if isinstance(x, tuple) else x for x in scratch],
        compiler_params=pltpu.CompilerParams(vmem_limit_bytes=VMEM_LIMIT),
        name=name,
    )(*operands)


def back_transform(x, pieces, sweep_ranges):
    count = lax.axis_size("row")
    place = jnp.stack([lax.axis_index("row"), lax.axis_index("col"), count]).astype(jnp.int32)
    phase = sweep_ranges[:, 0] % NB
    message = ((17 * ROWS, NB), F32)
    own, to_pair, to_other, high, low, x = call(
        inner_kernel, "inner_products",
        [(((OWN + 1) * ROWS, NB), F32), message, message, ((OWN * 64, NB), BF16), ((OWN * 64, NB), BF16), ((EIG, OWN * NB), F32)],
        [(SWEEPS, OWN * NB)],
        [place, sweep_ranges, x, *pieces],
    )
    within = [(i, i ^ 1) for i in range(count)]
    across = [(i, (i + 1) % count) for i in range(1, count, 2)]
    across = across + [(t, s) for s, t in across]
    pair = lax.ppermute(to_pair, "row", within)
    other = lax.ppermute(to_other, "row", across)
    out, = call(
        apply_kernel, "apply_sweeps",
        [((EIG, OWN * NB), F32)],
        [(EIG, OWN * NB), pltpu.SemaphoreType.DMA((OWN // PART,)), (NB * ROWS, NB), (SWEEPS * 32, NB), (SWEEPS * 32, NB), (SWEEPS * EIG, NB), (SWEEPS * 32, NB), (40 * 16, NB)]
        + [(2 * EIG, NB)] * (SWEEPS - WIDE) + [(EIG, NB)] * SWEEPS,
        [place, phase, own, pair, other, x, high, low],
        pl.ANY,
    )
    return out


def sweep_pieces(reflectors):
    cols, count = lax.axis_size("col"), lax.axis_size("row")
    width = count // cols
    groups = [[g * width + q for q in range(width)] for g in range(cols)]
    mine = lax.all_to_all(
        reflectors.reshape(width, -1), "row", split_axis=0, concat_axis=0, tiled=True,
        axis_index_groups=groups,
    )
    pieces = []
    for k in range(cols):
        pairs = [
            (c * count + g * width + q, ((g - k) % cols) * count + c * width + q)
            for c in range(cols) for g in range(cols) for q in range(width)
        ]
        pieces.append(lax.ppermute(mine, ("col", "row"), pairs))
    return pieces


def per_device(eigenvectors, reflectors, sweep_ranges):
    pieces = sweep_pieces(reflectors)
    x = lax.all_to_all(eigenvectors.reshape(2, -1, OWN * NB), "row", split_axis=1, concat_axis=1, tiled=True)
    x = x.transpose(1, 0, 2)
    return back_transform(x, pieces, sweep_ranges)


def solution(mesh):
    placed = (P(("col", "row"), None), P("row", "col"), P())
    return jax.shard_map(
        per_device, mesh=mesh, in_specs=placed, out_specs=P("col", "row"), check_vma=False
    )
```

```python
import jax
import jax.numpy as jnp
from jax import lax
from jax.experimental import pallas as pl
from jax.experimental.pallas import tpu as pltpu
from jax.sharding import PartitionSpec as P

NB = 128
SWEEPS = 32
OWN = 32
EIG = 64
HALO = 32
PART = 8
WIDE = 16
ROWS = 24
F32 = jnp.float32
BF16 = jnp.bfloat16
VMEM_LIMIT = 48 * 1024 * 1024


def split(x):
    high = x.astype(BF16)
    low = (x - high.astype(F32)).astype(BF16)
    return high, low


def halves(low, high):
    lane = lax.broadcasted_iota(jnp.int32, low.shape, 1)
    return jnp.where(lane < 64, pltpu.roll(low, NB - 16, 1), pltpu.roll(high, 48, 1))


def lane_group(rows):
    return lax.broadcasted_iota(jnp.int32, (rows, NB), 1) // 32


def sweep_bounds(ranges_ref):
    lower = jnp.broadcast_to(ranges_ref[:, 0:1], (SWEEPS, NB))
    upper = jnp.broadcast_to(ranges_ref[:, 1:2], (SWEEPS, NB))
    phase = lower & (NB - 1)
    first = lower >> 7
    last = (upper - phase - NB) >> 7
    return phase, first, last


def heads_tails(rows, bounds, block):
    phase, first, last = bounds
    lane = lax.broadcasted_iota(jnp.int32, (SWEEPS, NB), 1)
    head_on = (lane >= phase) & (block >= first) & (block <= last)
    tail_on = (lane < phase) & (block - 1 >= first) & (block - 1 <= last)
    return jnp.where(head_on, rows, 0.0), jnp.where(tail_on, rows, 0.0)


def fold(x, rows):
    group = lane_group(rows)
    turned = pltpu.roll(x, 32, 1)
    def keep(even, odd):
        parts = [(even if q % 2 == 0 else odd)[q * rows:(q + 1) * rows] for q in range(4)]
        out = parts[0]
        for q in range(1, 4):
            out = jnp.where(group == q, parts[q], out)
        return out
    return keep(x, turned), keep(turned, x)


def inner_products(x, right_high, right_low):
    left = jnp.concatenate(split(x), axis=1)
    right = jnp.concatenate([right_high] * 2 + [right_low] * 2, axis=0)
    right = jnp.concatenate([right, right], axis=1)
    prod = lax.dot_general(left, right, (((1,), (1,)), ((), ())), preferred_element_type=F32)
    return prod[:, :NB] + prod[:, NB:]


def outer_products(y, right_high, right_low):
    left = jnp.concatenate(split(y), axis=0)
    def four(both):
        return jnp.concatenate([both[:32]] * 4 + [both[32:]] * 4, axis=0)
    right = jnp.concatenate([four(right_high), four(right_low)], axis=1)
    prod = lax.dot_general(left, right, (((1,), (0,)), ((), ())), preferred_element_type=F32)
    prod = prod[:64] + prod[64:]
    return prod[:, :NB] + prod[:, NB:]


def needed(k):
    lane = lax.broadcasted_iota(jnp.int32, (ROWS, NB), 1) & 31
    return lane >= k - 1


def pack(ref, row_of, message):
    def block(k):
        return ref[pl.ds(row_of(k) * ROWS, ROWS)]

    message[pl.ds(0, ROWS)] = block(1)
    for k in range(2, 17):
        other = pltpu.roll(block(34 - k), NB - 33 + k, 1)
        message[pl.ds((k - 1) * ROWS, ROWS)] = jnp.where(needed(k), block(k), other)
    message[pl.ds(16 * ROWS, ROWS)] = block(17)


def unpack(message, valid=None):
    def block(m):
        data = message[pl.ds(m * ROWS, ROWS)]
        return data if valid is None else jnp.where(valid, data, 0.0)

    yield 1, block(0)
    for k in range(2, 17):
        both = block(k - 1)
        yield k, jnp.where(needed(k), both, 0.0)
        yield 34 - k, jnp.where(needed(34 - k), pltpu.roll(both, 33 - k, 1), 0.0)
    yield 17, jnp.where(needed(17), block(16), 0.0)


def inner_kernel(ranges_ref, arrived_ref, v0, v1, v2, v3,
                 out_ref, pair_ref, other_ref, high_ref, low_ref, x_ref, v_ref):
    for k, piece in enumerate((v0, v1, v2, v3)):
        first = pl.multiple_of(((lax.axis_index("col") + k) & 3) * 8, 8)
        v_ref[pl.ds(first, 8), :] = piece[...]
    bounds = sweep_bounds(ranges_ref)
    row = lax.broadcasted_iota(jnp.int32, (SWEEPS, NB), 0)
    lane = lax.broadcasted_iota(jnp.int32, (SWEEPS, NB), 1)
    upper = row <= (lane & 31)
    heads = (lane & 32) == 0
    place = lax.axis_index("row")
    base = place * OWN
    out_ref[pl.ds(0, ROWS)] = jnp.zeros((ROWS, NB), F32)
    for a in range(OWN):
        cols = pl.ds(a * NB, NB)
        head, tail = heads_tails(v_ref[:, cols], bounds, base + a)
        high, low = split(jnp.concatenate([head, tail], axis=0))
        high_ref[pl.ds(a * 64, 64)] = high
        low_ref[pl.ds(a * 64, 64)] = low
        x = arrived_ref[:, :, cols].reshape(EIG, NB)
        x_ref[:, cols] = x
        inner = inner_products(jnp.concatenate([x, head, tail], axis=0), high, low)
        of_head, of_tail = inner[64:96], inner[96:128]
        gram = jnp.where(upper == heads, of_head, of_tail)
        inner_head, inner_tail = fold(inner[:64], 16)
        gram_head, gram_tail = fold(gram, 8)
        out_ref[pl.ds((a + 1) * ROWS, 16)] = inner_head
        out_ref[pl.ds((a + 1) * ROWS + 16, 8)] = gram_head
        out_ref[pl.ds(a * ROWS, 16)] += inner_tail
        out_ref[pl.ds(a * ROWS + 16, 8)] += gram_tail

    def to_next(message):
        pack(out_ref, lambda k: 33 - k, message)

    def to_last(message):
        pack(out_ref, lambda k: k - 1, message)

    odd = place & 1

    @pl.when(odd == 0)
    def _():
        to_next(pair_ref)
        to_last(other_ref)

    @pl.when(odd == 1)
    def _():
        to_last(pair_ref)
        to_next(other_ref)


def apply_kernel(phase_ref, own_ref, pair_ref, other_ref, x_ref, high_ref, low_ref,
                 out_ref, result, sems, phase, phase_sem, gather, coef, coef_half, inner, inner_half, rows_t, *shifted):
    copy_phase = pltpu.make_async_copy(phase_ref, phase, phase_sem)
    copy_phase.start()

    def at(place, count=1):
        return pl.ds(place * ROWS, count * ROWS)

    gather[at(HALO, OWN)] = own_ref[at(1, OWN)]
    gather[at(2 * HALO + OWN - 1, 33)] = jnp.zeros((33 * ROWS, NB), F32)
    gather[at(HALO - 1)] = own_ref[at(0)]

    def take(low_blocks, high_blocks):
        for k, block in low_blocks:
            if k == 1:
                gather[at(HALO - 1)] += block
            else:
                gather[at(HALO - k)] = block
        for k, block in high_blocks:
            if k == 1:
                gather[at(HALO + OWN - 1)] += block
            else:
                gather[at(HALO + OWN - 2 + k)] = block

    place = lax.axis_index("row")
    odd = place & 1

    @pl.when(odd == 0)
    def _():
        take(unpack(other_ref, place > 0), unpack(pair_ref))

    @pl.when(odd == 1)
    def _():
        take(unpack(pair_ref), unpack(other_ref, place < lax.axis_size("row") - 1))

    for q in range(8):
        block = gather[pl.ds(16 + q, NB, stride=ROWS), :].T
        for g in range(4):
            coef[pl.ds((g * 8 + q) * 32, 32)] = block[g * 32:(g + 1) * 32]
    square = coef[pl.ds(0, SWEEPS, stride=33), :]
    all_tau = jnp.where(square > 0, 2.0 / jnp.where(square > 0, square, 1.0), 0.0)
    row = lax.broadcasted_iota(jnp.int32, (SWEEPS, NB), 0)
    for j in range(SWEEPS):
        mine = jnp.broadcast_to(all_tau[j:j + 1], (SWEEPS, NB))
        scaled = coef[pl.ds(j * 32, 32)] * jnp.where(row < j, all_tau, mine)
        coef[pl.ds(j * 32, 32)] = scaled
        count = 32 if j < WIDE else 16
        coef_half[pl.ds(j * 32, count)] = halves(scaled[:count], scaled[:count])

    for q in range(16):
        block = gather[pl.ds(q, NB, stride=ROWS), :].T
        parts = [block[g * 32:(g + 1) * 32] * all_tau for g in range(4)]
        for g in range(4):
            inner[pl.ds(g * 16 + q + 8 * EIG, 24, stride=64), :] = parts[g][8:]
        for g in range(2):
            inner_half[pl.ds(g * 16 + q, 16, stride=32), :] = halves(parts[g][:16], parts[g + 2][:16])

    copy_phase.wait()
    phases = [phase[j] for j in range(SWEEPS)]
    wide, half = shifted[:SWEEPS - WIDE], shifted[SWEEPS - WIDE:]
    lane = lax.broadcasted_iota(jnp.int32, (EIG // 2, NB), 1) & 63

    def keep_half(j, y):
        half[j][pl.ds(0, 32)] = jnp.where(lane == 0, 0.0, pltpu.roll(y, 1, 1))
        half[j][pl.ds(32, 32)] = jnp.where(lane == 63, 0.0, pltpu.roll(y, NB - 1, 1))

    for j in range(SWEEPS - 1, WIDE - 2, -1):
        total = inner[pl.ds(j * EIG, EIG)]
        for i in range(SWEEPS - 1, j, -1):
            same = coef[pl.ds(j * 32 + i, 1), :]
            next_to = coef[pl.ds(i * 32 + j, 1), :]
            start = pl.multiple_of(jnp.where(phases[j] < phases[i], 0, EIG), EIG)
            total = total - same * inner[pl.ds(i * EIG, EIG)] - next_to * wide[i - WIDE][pl.ds(start, EIG)]
        inner[pl.ds(j * EIG, EIG)] = total
        if j >= WIDE:
            wide[j - WIDE][pl.ds(0, EIG)] = pltpu.roll(total, 1, 1)
            wide[j - WIDE][pl.ds(EIG, EIG)] = pltpu.roll(total, NB - 1, 1)
        both = halves(total[:32], total[32:])
        inner_half[pl.ds(j * 32, 32)] = both
        keep_half(j, both)

    for j in range(WIDE - 2, -1, -1):
        total = inner_half[pl.ds(j * 32, 32)]
        for i in range(SWEEPS - 1, j, -1):
            same = coef_half[pl.ds(j * 32 + i, 1), :]
            next_to = coef_half[pl.ds(i * 32 + j, 1), :]
            start = pl.multiple_of(jnp.where(phases[j] < phases[i], 0, 32), 32)
            total = total - same * inner_half[pl.ds(i * 32, 32)] - next_to * half[i][pl.ds(start, 32)]
        inner_half[pl.ds(j * 32, 32)] = total
        if j > 0:
            keep_half(j, total)

    for t in range(8):
        parts = [inner_half[pl.ds(g * 16 + q * 8 + t, 32, stride=32), :] for q in range(2) for g in range(2)]
        block = jnp.concatenate(parts, axis=0).T
        for h in range(2):
            rows_t[pl.ds(h * 8 + t, 40, stride=16), :] = block[h * 64 + 8:h * 64 + 48]

    def copy_out(c):
        part = pl.ds(c * PART * NB, PART * NB)
        return pltpu.make_async_copy(result.at[:, part], out_ref.at[:, part], sems.at[c])

    group = lane_group(8)
    for a in range(OWN):
        cols = pl.ds(a * NB, NB)
        rows = pl.ds(a * 64, 64)
        of_head = rows_t[pl.ds((a + 8) * 16, 16)]
        of_tail = rows_t[pl.ds((a + 7) * 16, 16)]
        spread = [jnp.concatenate([jnp.where(group == q * 2 + g, y[h * 8:h * 8 + 8], 0.0)
                                   for h in range(2) for g in range(2) for q in range(2)], axis=0)
                  for y in (of_head, of_tail)]
        update = outer_products(jnp.concatenate(spread, axis=1), high_ref[rows], low_ref[rows])
        result[:, cols] = x_ref[:, cols] - update
        if (a + 1) % PART == 0:
            copy_out(a // PART).start()
    for c in range(OWN // PART):
        copy_out(c).wait()


def call(kernel, name, out_shape, scratch, operands, space=pltpu.VMEM):
    vmem = pl.BlockSpec(memory_space=pltpu.VMEM)
    any_space = pl.BlockSpec(memory_space=pl.ANY)
    specs = [any_space if x.ndim == 1 else vmem for x in operands]
    return pl.pallas_call(
        kernel,
        out_shape=tuple(jax.ShapeDtypeStruct(*x) for x in out_shape),
        in_specs=specs,
        out_specs=(pl.BlockSpec(memory_space=space),) * len(out_shape),
        scratch_shapes=[pltpu.VMEM(x, F32) if isinstance(x, tuple) else x for x in scratch],
        compiler_params=pltpu.CompilerParams(vmem_limit_bytes=VMEM_LIMIT),
        name=name,
    )(*operands)


def back_transform(x, pieces, sweep_ranges):
    count = lax.axis_size("row")
    phase = sweep_ranges[:, 0] % NB
    message = ((17 * ROWS, NB), F32)
    own, to_pair, to_other, high, low, x = call(
        inner_kernel, "inner_products",
        [(((OWN + 1) * ROWS, NB), F32), message, message, ((OWN * 64, NB), BF16), ((OWN * 64, NB), BF16), ((EIG, OWN * NB), F32)],
        [(SWEEPS, OWN * NB)],
        [sweep_ranges, x, *pieces],
    )
    within = [(i, i ^ 1) for i in range(count)]
    across = [(i, (i + 1) % count) for i in range(1, count, 2)]
    across = across + [(t, s) for s, t in across]
    pair = lax.ppermute(to_pair, "row", within)
    other = lax.ppermute(to_other, "row", across)
    out, = call(
        apply_kernel, "apply_sweeps",
        [((EIG, OWN * NB), F32)],
        [(EIG, OWN * NB), pltpu.SemaphoreType.DMA((OWN // PART,)),
         pltpu.SMEM((SWEEPS,), jnp.int32), pltpu.SemaphoreType.DMA, (NB * ROWS, NB), (SWEEPS * 32, NB), (SWEEPS * 32, NB), (SWEEPS * EIG, NB), (SWEEPS * 32, NB), (40 * 16, NB)]
        + [(2 * EIG, NB)] * (SWEEPS - WIDE) + [(EIG, NB)] * SWEEPS,
        [phase, own, pair, other, x, high, low],
        pl.ANY,
    )
    return out


def sweep_pieces(reflectors):
    cols, count = lax.axis_size("col"), lax.axis_size("row")
    width = count // cols
    groups = [[g * width + q for q in range(width)] for g in range(cols)]
    mine = lax.all_to_all(
        reflectors.reshape(width, -1), "row", split_axis=0, concat_axis=0, tiled=True,
        axis_index_groups=groups,
    )
    pieces = []
    for k in range(cols):
        pairs = [
            (c * count + g * width + q, ((g - k) % cols) * count + c * width + q)
            for c in range(cols) for g in range(cols) for q in range(width)
        ]
        pieces.append(lax.ppermute(mine, ("col", "row"), pairs))
    return pieces


def per_device(eigenvectors, reflectors, sweep_ranges):
    pieces = sweep_pieces(reflectors)
    x = lax.all_to_all(eigenvectors.reshape(2, -1, OWN * NB), "row", split_axis=1, concat_axis=1, tiled=True)
    x = x.transpose(1, 0, 2)
    return back_transform(x, pieces, sweep_ranges)


def solution(mesh):
    placed = (P(("col", "row"), None), P("row", "col"), P())
    return jax.shard_map(
        per_device, mesh=mesh, in_specs=placed, out_specs=P("col", "row"), check_vma=False
    )
```

```python
import jax
import jax.numpy as jnp
from jax import lax
from jax.experimental import pallas as pl
from jax.experimental.pallas import tpu as pltpu
from jax.sharding import PartitionSpec as P

NB = 128
SWEEPS = 32
OWN = 32
EIG = 64
HALO = 32
ENDS = (10, 18, 24, 28, 31, 32)
WIDE = 16
ROWS = 24
F32 = jnp.float32
BF16 = jnp.bfloat16
VMEM_LIMIT = 48 * 1024 * 1024


def split(x):
    high = x.astype(BF16)
    low = (x - high.astype(F32)).astype(BF16)
    return high, low


def halves(low, high):
    lane = lax.broadcasted_iota(jnp.int32, low.shape, 1)
    return jnp.where(lane < 64, pltpu.roll(low, NB - 16, 1), pltpu.roll(high, 48, 1))


def lane_group(rows):
    return lax.broadcasted_iota(jnp.int32, (rows, NB), 1) // 32


def sweep_bounds(ranges_ref):
    lower = jnp.broadcast_to(ranges_ref[:, 0:1], (SWEEPS, NB))
    upper = jnp.broadcast_to(ranges_ref[:, 1:2], (SWEEPS, NB))
    phase = lower & (NB - 1)
    first = lower >> 7
    last = (upper - phase - NB) >> 7
    return phase, first, last


def heads_tails(rows, bounds, block):
    phase, first, last = bounds
    lane = lax.broadcasted_iota(jnp.int32, (SWEEPS, NB), 1)
    head_on = (lane >= phase) & (block >= first) & (block <= last)
    tail_on = (lane < phase) & (block - 1 >= first) & (block - 1 <= last)
    return jnp.where(head_on, rows, 0.0), jnp.where(tail_on, rows, 0.0)


def fold(x, rows):
    group = lane_group(rows)
    turned = pltpu.roll(x, 32, 1)
    def keep(even, odd):
        parts = [(even if q % 2 == 0 else odd)[q * rows:(q + 1) * rows] for q in range(4)]
        out = parts[0]
        for q in range(1, 4):
            out = jnp.where(group == q, parts[q], out)
        return out
    return keep(x, turned), keep(turned, x)


def inner_products(x, both):
    left = jnp.concatenate(split(x), axis=1)
    right = jnp.concatenate(split(jnp.concatenate([both, both], axis=0).T), axis=1)
    right = jnp.concatenate([right, right], axis=0)
    prod = lax.dot_general(left, right, (((1,), (0,)), ((), ())), preferred_element_type=F32)
    return prod[:, :NB] + prod[:, NB:]


def outer_products(y, right_high, right_low):
    left = jnp.concatenate(split(y), axis=0)
    def four(both):
        return jnp.concatenate([both[:32]] * 4 + [both[32:]] * 4, axis=0)
    right = jnp.concatenate([four(right_high), four(right_low)], axis=1)
    prod = lax.dot_general(left, right, (((1,), (0,)), ((), ())), preferred_element_type=F32)
    prod = prod[:64] + prod[64:]
    return prod[:, :NB] + prod[:, NB:]


def needed(k):
    lane = lax.broadcasted_iota(jnp.int32, (ROWS, NB), 1) & 31
    return lane >= k - 1


def pack(ref, row_of, message):
    def block(k):
        return ref[pl.ds(row_of(k) * ROWS, ROWS)]

    message[pl.ds(0, ROWS)] = block(1)
    for k in range(2, 17):
        other = pltpu.roll(block(34 - k), NB - 33 + k, 1)
        message[pl.ds((k - 1) * ROWS, ROWS)] = jnp.where(needed(k), block(k), other)
    message[pl.ds(16 * ROWS, ROWS)] = block(17)


def unpack(message, valid=None):
    def block(m):
        data = message[pl.ds(m * ROWS, ROWS)]
        return data if valid is None else jnp.where(valid, data, 0.0)

    yield 1, block(0)
    for k in range(2, 17):
        both = block(k - 1)
        yield k, jnp.where(needed(k), both, 0.0)
        yield 34 - k, jnp.where(needed(34 - k), pltpu.roll(both, 33 - k, 1), 0.0)
    yield 17, jnp.where(needed(17), block(16), 0.0)


def inner_kernel(ranges_ref, arrived_ref, v0, v1, v2, v3,
                 out_ref, pair_ref, other_ref, high_ref, low_ref, x_ref, v_ref):
    for k, piece in enumerate((v0, v1, v2, v3)):
        first = pl.multiple_of(((lax.axis_index("col") + k) & 3) * 8, 8)
        v_ref[pl.ds(first, 8), :] = piece[...]
    bounds = sweep_bounds(ranges_ref)
    row = lax.broadcasted_iota(jnp.int32, (SWEEPS, NB), 0)
    lane = lax.broadcasted_iota(jnp.int32, (SWEEPS, NB), 1)
    upper = row <= (lane & 31)
    heads = (lane & 32) == 0
    place = lax.axis_index("row")
    base = place * OWN
    out_ref[pl.ds(0, ROWS)] = jnp.zeros((ROWS, NB), F32)
    for a in range(OWN):
        cols = pl.ds(a * NB, NB)
        head, tail = heads_tails(v_ref[:, cols], bounds, base + a)
        both = jnp.concatenate([head, tail], axis=0)
        high, low = split(both)
        high_ref[pl.ds(a * 64, 64)] = high
        low_ref[pl.ds(a * 64, 64)] = low
        x = arrived_ref[:, :, cols].reshape(EIG, NB)
        x_ref[:, cols] = x
        inner = inner_products(jnp.concatenate([x, both], axis=0), both)
        of_head, of_tail = inner[64:96], inner[96:128]
        gram = jnp.where(upper == heads, of_head, of_tail)
        inner_head, inner_tail = fold(inner[:64], 16)
        gram_head, gram_tail = fold(gram, 8)
        out_ref[pl.ds((a + 1) * ROWS, 16)] = inner_head
        out_ref[pl.ds((a + 1) * ROWS + 16, 8)] = gram_head
        out_ref[pl.ds(a * ROWS, 16)] += inner_tail
        out_ref[pl.ds(a * ROWS + 16, 8)] += gram_tail

    def to_next(message):
        pack(out_ref, lambda k: 33 - k, message)

    def to_last(message):
        pack(out_ref, lambda k: k - 1, message)

    odd = place & 1

    @pl.when(odd == 0)
    def _():
        to_next(pair_ref)
        to_last(other_ref)

    @pl.when(odd == 1)
    def _():
        to_last(pair_ref)
        to_next(other_ref)


def apply_kernel(phase_ref, own_ref, pair_ref, other_ref, x_ref, high_ref, low_ref,
                 out_ref, result, sems, phase, phase_sem, gather, coef, coef_half, inner, inner_half, rows_t, *shifted):
    copy_phase = pltpu.make_async_copy(phase_ref, phase, phase_sem)
    copy_phase.start()

    def at(place, count=1):
        return pl.ds(place * ROWS, count * ROWS)

    gather[at(HALO, OWN)] = own_ref[at(1, OWN)]
    gather[at(2 * HALO + OWN - 1, 33)] = jnp.zeros((33 * ROWS, NB), F32)
    gather[at(HALO - 1)] = own_ref[at(0)]

    def take(low_blocks, high_blocks):
        for k, block in low_blocks:
            if k == 1:
                gather[at(HALO - 1)] += block
            else:
                gather[at(HALO - k)] = block
        for k, block in high_blocks:
            if k == 1:
                gather[at(HALO + OWN - 1)] += block
            else:
                gather[at(HALO + OWN - 2 + k)] = block

    place = lax.axis_index("row")
    odd = place & 1

    @pl.when(odd == 0)
    def _():
        take(unpack(other_ref, place > 0), unpack(pair_ref))

    @pl.when(odd == 1)
    def _():
        take(unpack(pair_ref), unpack(other_ref, place < lax.axis_size("row") - 1))

    for q in range(8):
        block = gather[pl.ds(16 + q, NB, stride=ROWS), :].T
        for g in range(4):
            coef[pl.ds((g * 8 + q) * 32, 32)] = block[g * 32:(g + 1) * 32]
    square = coef[pl.ds(0, SWEEPS, stride=33), :]
    all_tau = jnp.where(square > 0, 2.0 / jnp.where(square > 0, square, 1.0), 0.0)
    row = lax.broadcasted_iota(jnp.int32, (SWEEPS, NB), 0)
    for j in range(SWEEPS):
        mine = jnp.broadcast_to(all_tau[j:j + 1], (SWEEPS, NB))
        scaled = coef[pl.ds(j * 32, 32)] * jnp.where(row < j, all_tau, mine)
        coef[pl.ds(j * 32, 32)] = scaled
        count = 32 if j < WIDE else 16
        coef_half[pl.ds(j * 32, count)] = halves(scaled[:count], scaled[:count])

    for q in range(16):
        block = gather[pl.ds(q, NB, stride=ROWS), :].T
        parts = [block[g * 32:(g + 1) * 32] * all_tau for g in range(4)]
        for g in range(4):
            inner[pl.ds(g * 16 + q + 8 * EIG, 24, stride=64), :] = parts[g][8:]
        for g in range(2):
            inner_half[pl.ds(g * 16 + q, 16, stride=32), :] = halves(parts[g][:16], parts[g + 2][:16])

    copy_phase.wait()
    phases = [phase[j] for j in range(SWEEPS)]
    wide, half = shifted[:SWEEPS - WIDE], shifted[SWEEPS - WIDE:]
    lane = lax.broadcasted_iota(jnp.int32, (EIG // 2, NB), 1) & 63

    def keep_half(j, y):
        half[j][pl.ds(0, 32)] = jnp.where(lane == 0, 0.0, pltpu.roll(y, 1, 1))
        half[j][pl.ds(32, 32)] = jnp.where(lane == 63, 0.0, pltpu.roll(y, NB - 1, 1))

    for j in range(SWEEPS - 1, WIDE - 2, -1):
        total = inner[pl.ds(j * EIG, EIG)]
        for i in range(SWEEPS - 1, j, -1):
            same = coef[pl.ds(j * 32 + i, 1), :]
            next_to = coef[pl.ds(i * 32 + j, 1), :]
            start = pl.multiple_of(jnp.where(phases[j] < phases[i], 0, EIG), EIG)
            total = total - same * inner[pl.ds(i * EIG, EIG)] - next_to * wide[i - WIDE][pl.ds(start, EIG)]
        inner[pl.ds(j * EIG, EIG)] = total
        if j >= WIDE:
            wide[j - WIDE][pl.ds(0, EIG)] = pltpu.roll(total, 1, 1)
            wide[j - WIDE][pl.ds(EIG, EIG)] = pltpu.roll(total, NB - 1, 1)
        both = halves(total[:32], total[32:])
        inner_half[pl.ds(j * 32, 32)] = both
        keep_half(j, both)

    for j in range(WIDE - 2, -1, -1):
        total = inner_half[pl.ds(j * 32, 32)]
        for i in range(SWEEPS - 1, j, -1):
            same = coef_half[pl.ds(j * 32 + i, 1), :]
            next_to = coef_half[pl.ds(i * 32 + j, 1), :]
            start = pl.multiple_of(jnp.where(phases[j] < phases[i], 0, 32), 32)
            total = total - same * inner_half[pl.ds(i * 32, 32)] - next_to * half[i][pl.ds(start, 32)]
        inner_half[pl.ds(j * 32, 32)] = total
        if j > 0:
            keep_half(j, total)

    for t in range(8):
        parts = [inner_half[pl.ds(g * 16 + q * 8 + t, 32, stride=32), :] for q in range(2) for g in range(2)]
        block = jnp.concatenate(parts, axis=0).T
        for h in range(2):
            rows_t[pl.ds(h * 8 + t, 40, stride=16), :] = block[h * 64 + 8:h * 64 + 48]

    def copy_out(c):
        first = 0 if c == 0 else ENDS[c - 1]
        part = pl.ds(first * NB, (ENDS[c] - first) * NB)
        return pltpu.make_async_copy(result.at[:, part], out_ref.at[:, part], sems.at[c])

    group = lane_group(8)
    for a in range(OWN):
        cols = pl.ds(a * NB, NB)
        rows = pl.ds(a * 64, 64)
        of_head = rows_t[pl.ds((a + 8) * 16, 16)]
        of_tail = rows_t[pl.ds((a + 7) * 16, 16)]
        spread = [jnp.concatenate([jnp.where(group == q * 2 + g, y[h * 8:h * 8 + 8], 0.0)
                                   for h in range(2) for g in range(2) for q in range(2)], axis=0)
                  for y in (of_head, of_tail)]
        update = outer_products(jnp.concatenate(spread, axis=1), high_ref[rows], low_ref[rows])
        result[:, cols] = x_ref[:, cols] - update
        if a + 1 in ENDS:
            copy_out(ENDS.index(a + 1)).start()
    for c in range(len(ENDS)):
        copy_out(c).wait()


def call(kernel, name, out_shape, scratch, operands, space=pltpu.VMEM):
    vmem = pl.BlockSpec(memory_space=pltpu.VMEM)
    any_space = pl.BlockSpec(memory_space=pl.ANY)
    specs = [any_space if x.ndim == 1 else vmem for x in operands]
    return pl.pallas_call(
        kernel,
        out_shape=tuple(jax.ShapeDtypeStruct(*x) for x in out_shape),
        in_specs=specs,
        out_specs=(pl.BlockSpec(memory_space=space),) * len(out_shape),
        scratch_shapes=[pltpu.VMEM(x, F32) if isinstance(x, tuple) else x for x in scratch],
        compiler_params=pltpu.CompilerParams(vmem_limit_bytes=VMEM_LIMIT),
        name=name,
    )(*operands)


def back_transform(x, pieces, sweep_ranges):
    count = lax.axis_size("row")
    phase = sweep_ranges[:, 0] % NB
    message = ((17 * ROWS, NB), F32)
    own, to_pair, to_other, high, low, x = call(
        inner_kernel, "inner_products",
        [(((OWN + 1) * ROWS, NB), F32), message, message, ((OWN * 64, NB), BF16), ((OWN * 64, NB), BF16), ((EIG, OWN * NB), F32)],
        [(SWEEPS, OWN * NB)],
        [sweep_ranges, x, *pieces],
    )
    within = [(i, i ^ 1) for i in range(count)]
    across = [(i, (i + 1) % count) for i in range(1, count, 2)]
    across = across + [(t, s) for s, t in across]
    pair = lax.ppermute(to_pair, "row", within)
    other = lax.ppermute(to_other, "row", across)
    out, = call(
        apply_kernel, "apply_sweeps",
        [((EIG, OWN * NB), F32)],
        [(EIG, OWN * NB), pltpu.SemaphoreType.DMA((len(ENDS),)),
         pltpu.SMEM((SWEEPS,), jnp.int32), pltpu.SemaphoreType.DMA, (NB * ROWS, NB), (SWEEPS * 32, NB), (SWEEPS * 32, NB), (SWEEPS * EIG, NB), (SWEEPS * 32, NB), (40 * 16, NB)]
        + [(2 * EIG, NB)] * (SWEEPS - WIDE) + [(EIG, NB)] * SWEEPS,
        [phase, own, pair, other, x, high, low],
        pl.ANY,
    )
    return out


def sweep_pieces(reflectors):
    cols, count = lax.axis_size("col"), lax.axis_size("row")
    width = count // cols
    groups = [[g * width + q for q in range(width)] for g in range(cols)]
    mine = lax.all_to_all(
        reflectors.reshape(width, -1), "row", split_axis=0, concat_axis=0, tiled=True,
        axis_index_groups=groups,
    )
    pieces = []
    for k in range(cols):
        pairs = [
            (c * count + g * width + q, ((g - k) % cols) * count + c * width + q)
            for c in range(cols) for g in range(cols) for q in range(width)
        ]
        pieces.append(lax.ppermute(mine, ("col", "row"), pairs))
    return pieces


def per_device(eigenvectors, reflectors, sweep_ranges):
    pieces = sweep_pieces(reflectors)
    x = lax.all_to_all(eigenvectors.reshape(2, -1, OWN * NB), "row", split_axis=1, concat_axis=1, tiled=True)
    x = x.transpose(1, 0, 2)
    return back_transform(x, pieces, sweep_ranges)


def solution(mesh):
    placed = (P(("col", "row"), None), P("row", "col"), P())
    return jax.shard_map(
        per_device, mesh=mesh, in_specs=placed, out_specs=P("col", "row"), check_vma=False
    )
```

```python
import jax
import jax.numpy as jnp
from jax import lax
from jax.experimental import pallas as pl
from jax.experimental.pallas import tpu as pltpu
from jax.sharding import PartitionSpec as P

NB = 128
SWEEPS = 32
OWN = 32
EIG = 64
HALO = 32
ENDS = (10, 18, 24, 28, 31, 32)
WIDE = 16
ROWS = 24
F32 = jnp.float32
BF16 = jnp.bfloat16
VMEM_LIMIT = 48 * 1024 * 1024


def split(x):
    high = x.astype(BF16)
    low = (x - high.astype(F32)).astype(BF16)
    return high, low


def halves(low, high):
    lane = lax.broadcasted_iota(jnp.int32, low.shape, 1)
    return jnp.where(lane < 64, pltpu.roll(low, NB - 16, 1), pltpu.roll(high, 48, 1))


def lane_group(rows):
    return lax.broadcasted_iota(jnp.int32, (rows, NB), 1) // 32


def sweep_bounds(ranges_ref):
    lower = jnp.broadcast_to(ranges_ref[:, 0:1], (SWEEPS, NB))
    upper = jnp.broadcast_to(ranges_ref[:, 1:2], (SWEEPS, NB))
    phase = lower & (NB - 1)
    first = lower >> 7
    last = (upper - phase - NB) >> 7
    return phase, first, last


def active(bounds, block):
    _, first, last = bounds
    return (block >= first) & (block <= last)


def fold(x, rows):
    group = lane_group(rows)
    turned = pltpu.roll(x, 32, 1)
    def keep(even, odd):
        parts = [(even if q % 2 == 0 else odd)[q * rows:(q + 1) * rows] for q in range(4)]
        out = parts[0]
        for q in range(1, 4):
            out = jnp.where(group == q, parts[q], out)
        return out
    return keep(x, turned), keep(turned, x)


def inner_products(x, both):
    left = jnp.concatenate(split(x), axis=1)
    right = jnp.concatenate(split(jnp.concatenate([both, both], axis=0).T), axis=1)
    right = jnp.concatenate([right, right], axis=0)
    prod = lax.dot_general(left, right, (((1,), (0,)), ((), ())), preferred_element_type=F32)
    return prod[:, :NB] + prod[:, NB:]


def outer_products(y, right_high, right_low):
    left = jnp.concatenate(split(y), axis=0)
    def four(both):
        return jnp.concatenate([both[:32]] * 4 + [both[32:]] * 4, axis=0)
    right = jnp.concatenate([four(right_high), four(right_low)], axis=1)
    prod = lax.dot_general(left, right, (((1,), (0,)), ((), ())), preferred_element_type=F32)
    prod = prod[:64] + prod[64:]
    return prod[:, :NB] + prod[:, NB:]


def needed(k):
    lane = lax.broadcasted_iota(jnp.int32, (ROWS, NB), 1) & 31
    return lane >= k - 1


def pack(ref, row_of, message):
    def block(k):
        return ref[pl.ds(row_of(k) * ROWS, ROWS)]

    message[pl.ds(0, ROWS)] = block(1)
    for k in range(2, 17):
        other = pltpu.roll(block(34 - k), NB - 33 + k, 1)
        message[pl.ds((k - 1) * ROWS, ROWS)] = jnp.where(needed(k), block(k), other)
    message[pl.ds(16 * ROWS, ROWS)] = block(17)


def unpack(message, valid=None):
    def block(m):
        data = message[pl.ds(m * ROWS, ROWS)]
        return data if valid is None else jnp.where(valid, data, 0.0)

    yield 1, block(0)
    for k in range(2, 17):
        both = block(k - 1)
        yield k, jnp.where(needed(k), both, 0.0)
        yield 34 - k, jnp.where(needed(34 - k), pltpu.roll(both, 33 - k, 1), 0.0)
    yield 17, jnp.where(needed(17), block(16), 0.0)


def inner_kernel(ranges_ref, arrived_ref, v0, v1, v2, v3,
                 out_ref, pair_ref, other_ref, high_ref, low_ref, x_ref, v_ref):
    for k, piece in enumerate((v0, v1, v2, v3)):
        first = pl.multiple_of(((lax.axis_index("col") + k) & 3) * 8, 8)
        v_ref[pl.ds(first, 8), :] = piece[...]
    bounds = sweep_bounds(ranges_ref)
    row = lax.broadcasted_iota(jnp.int32, (SWEEPS, NB), 0)
    lane = lax.broadcasted_iota(jnp.int32, (SWEEPS, NB), 1)
    upper = row <= (lane & 31)
    heads = (lane & 32) == 0
    place = lax.axis_index("row")
    base = place * OWN
    head_lane, tail_lane = lane >= bounds[0], lane < bounds[0]
    before = active(bounds, base - 1)
    out_ref[pl.ds(0, ROWS)] = jnp.zeros((ROWS, NB), F32)
    for a in range(OWN):
        cols = pl.ds(a * NB, NB)
        here = active(bounds, base + a)
        rows = v_ref[:, cols]
        head = jnp.where(head_lane & here, rows, 0.0)
        tail = jnp.where(tail_lane & before, rows, 0.0)
        before = here
        both = jnp.concatenate([head, tail], axis=0)
        high, low = split(both)
        high_ref[pl.ds(a * 64, 64)] = high
        low_ref[pl.ds(a * 64, 64)] = low
        x = arrived_ref[:, :, cols].reshape(EIG, NB)
        x_ref[:, cols] = x
        inner = inner_products(jnp.concatenate([x, both], axis=0), both)
        of_head, of_tail = inner[64:96], inner[96:128]
        gram = jnp.where(upper == heads, of_head, of_tail)
        inner_head, inner_tail = fold(inner[:64], 16)
        gram_head, gram_tail = fold(gram, 8)
        out_ref[pl.ds((a + 1) * ROWS, 16)] = inner_head
        out_ref[pl.ds((a + 1) * ROWS + 16, 8)] = gram_head
        out_ref[pl.ds(a * ROWS, 16)] += inner_tail
        out_ref[pl.ds(a * ROWS + 16, 8)] += gram_tail

    def to_next(message):
        pack(out_ref, lambda k: 33 - k, message)

    def to_last(message):
        pack(out_ref, lambda k: k - 1, message)

    odd = place & 1

    @pl.when(odd == 0)
    def _():
        to_next(pair_ref)
        to_last(other_ref)

    @pl.when(odd == 1)
    def _():
        to_last(pair_ref)
        to_next(other_ref)


def apply_kernel(phase_ref, own_ref, pair_ref, other_ref, x_ref, high_ref, low_ref,
                 out_ref, result, sems, phase, phase_sem, gather, coef, coef_half, inner, inner_half, rows_t, *shifted):
    copy_phase = pltpu.make_async_copy(phase_ref, phase, phase_sem)
    copy_phase.start()

    def at(place, count=1):
        return pl.ds(place * ROWS, count * ROWS)

    gather[at(HALO, OWN)] = own_ref[at(1, OWN)]
    gather[at(2 * HALO + OWN - 1, 33)] = jnp.zeros((33 * ROWS, NB), F32)
    gather[at(HALO - 1)] = own_ref[at(0)]

    def take(low_blocks, high_blocks):
        for k, block in low_blocks:
            if k == 1:
                gather[at(HALO - 1)] += block
            else:
                gather[at(HALO - k)] = block
        for k, block in high_blocks:
            if k == 1:
                gather[at(HALO + OWN - 1)] += block
            else:
                gather[at(HALO + OWN - 2 + k)] = block

    place = lax.axis_index("row")
    odd = place & 1

    @pl.when(odd == 0)
    def _():
        take(unpack(other_ref, place > 0), unpack(pair_ref))

    @pl.when(odd == 1)
    def _():
        take(unpack(pair_ref), unpack(other_ref, place < lax.axis_size("row") - 1))

    for q in range(8):
        block = gather[pl.ds(16 + q, NB, stride=ROWS), :].T
        for g in range(4):
            coef[pl.ds((g * 8 + q) * 32, 32)] = block[g * 32:(g + 1) * 32]
    square = coef[pl.ds(0, SWEEPS, stride=33), :]
    all_tau = jnp.where(square > 0, 2.0 / jnp.where(square > 0, square, 1.0), 0.0)
    row = lax.broadcasted_iota(jnp.int32, (SWEEPS, NB), 0)
    for j in range(SWEEPS):
        mine = jnp.broadcast_to(all_tau[j:j + 1], (SWEEPS, NB))
        scaled = coef[pl.ds(j * 32, 32)] * jnp.where(row < j, all_tau, mine)
        coef[pl.ds(j * 32, 32)] = scaled
        count = 32 if j < WIDE else 16
        coef_half[pl.ds(j * 32, count)] = halves(scaled[:count], scaled[:count])

    for q in range(16):
        block = gather[pl.ds(q, NB, stride=ROWS), :].T
        parts = [block[g * 32:(g + 1) * 32] * all_tau for g in range(4)]
        for g in range(4):
            inner[pl.ds(g * 16 + q + 8 * EIG, 24, stride=64), :] = parts[g][8:]
        for g in range(2):
            inner_half[pl.ds(g * 16 + q, 16, stride=32), :] = halves(parts[g][:16], parts[g + 2][:16])

    copy_phase.wait()
    phases = [phase[j] for j in range(SWEEPS)]
    wide, half = shifted[:SWEEPS - WIDE], shifted[SWEEPS - WIDE:]
    lane = lax.broadcasted_iota(jnp.int32, (EIG // 2, NB), 1) & 63

    def keep_half(j, y):
        half[j][pl.ds(0, 32)] = jnp.where(lane == 0, 0.0, pltpu.roll(y, 1, 1))
        half[j][pl.ds(32, 32)] = jnp.where(lane == 63, 0.0, pltpu.roll(y, NB - 1, 1))

    for j in range(SWEEPS - 1, WIDE - 2, -1):
        total = inner[pl.ds(j * EIG, EIG)]
        for i in range(SWEEPS - 1, j, -1):
            same = coef[pl.ds(j * 32 + i, 1), :]
            next_to = coef[pl.ds(i * 32 + j, 1), :]
            start = pl.multiple_of(jnp.where(phases[j] < phases[i], 0, EIG), EIG)
            total = total - same * inner[pl.ds(i * EIG, EIG)] - next_to * wide[i - WIDE][pl.ds(start, EIG)]
        inner[pl.ds(j * EIG, EIG)] = total
        if j >= WIDE:
            wide[j - WIDE][pl.ds(0, EIG)] = pltpu.roll(total, 1, 1)
            wide[j - WIDE][pl.ds(EIG, EIG)] = pltpu.roll(total, NB - 1, 1)
        both = halves(total[:32], total[32:])
        inner_half[pl.ds(j * 32, 32)] = both
        keep_half(j, both)

    for j in range(WIDE - 2, -1, -1):
        total = inner_half[pl.ds(j * 32, 32)]
        for i in range(SWEEPS - 1, j, -1):
            same = coef_half[pl.ds(j * 32 + i, 1), :]
            next_to = coef_half[pl.ds(i * 32 + j, 1), :]
            start = pl.multiple_of(jnp.where(phases[j] < phases[i], 0, 32), 32)
            total = total - same * inner_half[pl.ds(i * 32, 32)] - next_to * half[i][pl.ds(start, 32)]
        inner_half[pl.ds(j * 32, 32)] = total
        if j > 0:
            keep_half(j, total)

    for t in range(8):
        parts = [inner_half[pl.ds(g * 16 + q * 8 + t, 32, stride=32), :] for q in range(2) for g in range(2)]
        block = jnp.concatenate(parts, axis=0).T
        for h in range(2):
            rows_t[pl.ds(h * 8 + t, 40, stride=16), :] = block[h * 64 + 8:h * 64 + 48]

    def copy_out(c):
        first = 0 if c == 0 else ENDS[c - 1]
        part = pl.ds(first * NB, (ENDS[c] - first) * NB)
        return pltpu.make_async_copy(result.at[:, part], out_ref.at[:, part], sems.at[c])

    group = lane_group(8)
    for a in range(OWN):
        cols = pl.ds(a * NB, NB)
        rows = pl.ds(a * 64, 64)
        of_head = rows_t[pl.ds((a + 8) * 16, 16)]
        of_tail = rows_t[pl.ds((a + 7) * 16, 16)]
        spread = [jnp.concatenate([jnp.where(group == q * 2 + g, y[h * 8:h * 8 + 8], 0.0)
                                   for h in range(2) for g in range(2) for q in range(2)], axis=0)
                  for y in (of_head, of_tail)]
        update = outer_products(jnp.concatenate(spread, axis=1), high_ref[rows], low_ref[rows])
        result[:, cols] = x_ref[:, cols] - update
        if a + 1 in ENDS:
            copy_out(ENDS.index(a + 1)).start()
    for c in range(len(ENDS)):
        copy_out(c).wait()


def call(kernel, name, out_shape, scratch, operands, space=pltpu.VMEM):
    vmem = pl.BlockSpec(memory_space=pltpu.VMEM)
    any_space = pl.BlockSpec(memory_space=pl.ANY)
    specs = [any_space if x.ndim == 1 else vmem for x in operands]
    return pl.pallas_call(
        kernel,
        out_shape=tuple(jax.ShapeDtypeStruct(*x) for x in out_shape),
        in_specs=specs,
        out_specs=(pl.BlockSpec(memory_space=space),) * len(out_shape),
        scratch_shapes=[pltpu.VMEM(x, F32) if isinstance(x, tuple) else x for x in scratch],
        compiler_params=pltpu.CompilerParams(vmem_limit_bytes=VMEM_LIMIT),
        name=name,
    )(*operands)


def back_transform(x, pieces, sweep_ranges):
    count = lax.axis_size("row")
    phase = sweep_ranges[:, 0] % NB
    message = ((17 * ROWS, NB), F32)
    own, to_pair, to_other, high, low, x = call(
        inner_kernel, "inner_products",
        [(((OWN + 1) * ROWS, NB), F32), message, message, ((OWN * 64, NB), BF16), ((OWN * 64, NB), BF16), ((EIG, OWN * NB), F32)],
        [(SWEEPS, OWN * NB)],
        [sweep_ranges, x, *pieces],
    )
    within = [(i, i ^ 1) for i in range(count)]
    across = [(i, (i + 1) % count) for i in range(1, count, 2)]
    across = across + [(t, s) for s, t in across]
    pair = lax.ppermute(to_pair, "row", within)
    other = lax.ppermute(to_other, "row", across)
    out, = call(
        apply_kernel, "apply_sweeps",
        [((EIG, OWN * NB), F32)],
        [(EIG, OWN * NB), pltpu.SemaphoreType.DMA((len(ENDS),)),
         pltpu.SMEM((SWEEPS,), jnp.int32), pltpu.SemaphoreType.DMA, (NB * ROWS, NB), (SWEEPS * 32, NB), (SWEEPS * 32, NB), (SWEEPS * EIG, NB), (SWEEPS * 32, NB), (40 * 16, NB)]
        + [(2 * EIG, NB)] * (SWEEPS - WIDE) + [(EIG, NB)] * SWEEPS,
        [phase, own, pair, other, x, high, low],
        pl.ANY,
    )
    return out


def sweep_pieces(reflectors):
    cols, count = lax.axis_size("col"), lax.axis_size("row")
    width = count // cols
    groups = [[g * width + q for q in range(width)] for g in range(cols)]
    mine = lax.all_to_all(
        reflectors.reshape(width, -1), "row", split_axis=0, concat_axis=0, tiled=True,
        axis_index_groups=groups,
    )
    pieces = []
    for k in range(cols):
        pairs = [
            (c * count + g * width + q, ((g - k) % cols) * count + c * width + q)
            for c in range(cols) for g in range(cols) for q in range(width)
        ]
        pieces.append(lax.ppermute(mine, ("col", "row"), pairs))
    return pieces


def per_device(eigenvectors, reflectors, sweep_ranges):
    pieces = sweep_pieces(reflectors)
    x = lax.all_to_all(eigenvectors.reshape(2, -1, OWN * NB), "row", split_axis=1, concat_axis=1, tiled=True)
    x = x.transpose(1, 0, 2)
    return back_transform(x, pieces, sweep_ranges)


def solution(mesh):
    placed = (P(("col", "row"), None), P("row", "col"), P())
    return jax.shard_map(
        per_device, mesh=mesh, in_specs=placed, out_specs=P("col", "row"), check_vma=False
    )
```

```python
import jax
import jax.numpy as jnp
from jax import lax
from jax.experimental import pallas as pl
from jax.experimental.pallas import tpu as pltpu
from jax.sharding import PartitionSpec as P

NB = 128
SWEEPS = 32
OWN = 32
EIG = 64
HALO = 32
ENDS = (10, 18, 24, 28, 31, 32)
WIDE = 16
ROWS = 24
F32 = jnp.float32
BF16 = jnp.bfloat16
VMEM_LIMIT = 48 * 1024 * 1024


def split(x):
    high = x.astype(BF16)
    low = (x - high.astype(F32)).astype(BF16)
    return high, low


def halves(low, high):
    lane = lax.broadcasted_iota(jnp.int32, low.shape, 1)
    return jnp.where(lane < 64, pltpu.roll(low, NB - 16, 1), pltpu.roll(high, 48, 1))


def lane_group(rows):
    return lax.broadcasted_iota(jnp.int32, (rows, NB), 1) // 32


def sweep_bounds(ranges_ref):
    lower = jnp.broadcast_to(ranges_ref[:, 0:1], (SWEEPS, NB))
    upper = jnp.broadcast_to(ranges_ref[:, 1:2], (SWEEPS, NB))
    phase = lower & (NB - 1)
    first = lower >> 7
    last = (upper - phase - NB) >> 7
    return phase, first, last


def active(bounds, block):
    _, first, last = bounds
    return (block >= first) & (block <= last)


def fold(x, rows):
    group = lane_group(rows)
    turned = pltpu.roll(x, 32, 1)
    def keep(even, odd):
        parts = [(even if q % 2 == 0 else odd)[q * rows:(q + 1) * rows] for q in range(4)]
        out = parts[0]
        for q in range(1, 4):
            out = jnp.where(group == q, parts[q], out)
        return out
    return keep(x, turned), keep(turned, x)


def inner_products(x, both):
    left = jnp.concatenate(split(x), axis=1)
    right = jnp.concatenate(split(jnp.concatenate([both, both], axis=0).T), axis=1)
    right = jnp.concatenate([right, right], axis=0)
    prod = lax.dot_general(left, right, (((1,), (0,)), ((), ())), preferred_element_type=F32)
    return prod[:, :NB] + prod[:, NB:]


def outer_products(y, right_high, right_low):
    left = jnp.concatenate(split(y), axis=0)
    def four(both):
        return jnp.concatenate([both[:32]] * 4 + [both[32:]] * 4, axis=0)
    right = jnp.concatenate([four(right_high), four(right_low)], axis=1)
    prod = lax.dot_general(left, right, (((1,), (0,)), ((), ())), preferred_element_type=F32)
    prod = prod[:64] + prod[64:]
    return prod[:, :NB] + prod[:, NB:]


def needed(k):
    lane = lax.broadcasted_iota(jnp.int32, (ROWS, NB), 1) & 31
    return lane >= k - 1


def pack(ref, row_of, message):
    def block(k):
        return ref[pl.ds(row_of(k) * ROWS, ROWS)]

    message[pl.ds(0, ROWS)] = block(1)
    for k in range(2, 17):
        other = pltpu.roll(block(34 - k), NB - 33 + k, 1)
        message[pl.ds((k - 1) * ROWS, ROWS)] = jnp.where(needed(k), block(k), other)
    message[pl.ds(16 * ROWS, ROWS)] = block(17)


def unpack(message, valid=None):
    def block(m):
        data = message[pl.ds(m * ROWS, ROWS)]
        return data if valid is None else jnp.where(valid, data, 0.0)

    yield 1, block(0)
    for k in range(2, 17):
        both = block(k - 1)
        yield k, jnp.where(needed(k), both, 0.0)
        yield 34 - k, jnp.where(needed(34 - k), pltpu.roll(both, 33 - k, 1), 0.0)
    yield 17, jnp.where(needed(17), block(16), 0.0)


def inner_kernel(ranges_ref, arrived_ref, v0, v1, v2, v3,
                 out_ref, pair_ref, other_ref, high_ref, low_ref, x_ref, v_ref):
    for k, piece in enumerate((v0, v1, v2, v3)):
        first = pl.multiple_of(((lax.axis_index("col") + k) & 3) * 8, 8)
        v_ref[pl.ds(first, 8), :] = piece[...]
    bounds = sweep_bounds(ranges_ref)
    row = lax.broadcasted_iota(jnp.int32, (SWEEPS, NB), 0)
    lane = lax.broadcasted_iota(jnp.int32, (SWEEPS, NB), 1)
    upper = row <= (lane & 31)
    heads = (lane & 32) == 0
    place = lax.axis_index("row")
    base = place * OWN
    head_lane, tail_lane = lane >= bounds[0], lane < bounds[0]
    before = active(bounds, base - 1)
    out_ref[pl.ds(0, ROWS)] = jnp.zeros((ROWS, NB), F32)
    for a in range(OWN):
        cols = pl.ds(a * NB, NB)
        here = active(bounds, base + a)
        rows = v_ref[:, cols]
        head = jnp.where(head_lane & here, rows, 0.0)
        tail = jnp.where(tail_lane & before, rows, 0.0)
        before = here
        both = jnp.concatenate([head, tail], axis=0)
        high, low = split(both)
        high_ref[pl.ds(a * 64, 64)] = high
        low_ref[pl.ds(a * 64, 64)] = low
        x = arrived_ref[:, :, cols].reshape(EIG, NB)
        x_ref[:, cols] = x
        inner = inner_products(jnp.concatenate([x, both], axis=0), both)
        of_head, of_tail = inner[64:96], inner[96:128]
        gram = jnp.where(upper == heads, of_head, of_tail)
        inner_head, inner_tail = fold(inner[:64], 16)
        gram_head, gram_tail = fold(gram, 8)
        out_ref[pl.ds((a + 1) * ROWS, 16)] = inner_head
        out_ref[pl.ds((a + 1) * ROWS + 16, 8)] = gram_head
        out_ref[pl.ds(a * ROWS, 16)] += inner_tail
        out_ref[pl.ds(a * ROWS + 16, 8)] += gram_tail

    def to_next(message):
        pack(out_ref, lambda k: 33 - k, message)

    def to_last(message):
        pack(out_ref, lambda k: k - 1, message)

    odd = place & 1

    @pl.when(odd == 0)
    def _():
        to_next(pair_ref)
        to_last(other_ref)

    @pl.when(odd == 1)
    def _():
        to_last(pair_ref)
        to_next(other_ref)


def apply_kernel(phase_ref, own_ref, pair_ref, other_ref, x_ref, high_ref, low_ref,
                 out_ref, result, sems, phase, phase_sem, gather, coef, coef_half, inner, inner_half, rows_t, *shifted):
    copy_phase = pltpu.make_async_copy(phase_ref, phase, phase_sem)
    copy_phase.start()

    def at(place, count=1):
        return pl.ds(place * ROWS, count * ROWS)

    gather[at(HALO, OWN)] = own_ref[at(1, OWN)]
    gather[at(2 * HALO + OWN - 1, 33)] = jnp.zeros((33 * ROWS, NB), F32)
    gather[at(HALO - 1)] = own_ref[at(0)]

    def take(low_blocks, high_blocks):
        for k, block in low_blocks:
            if k == 1:
                gather[at(HALO - 1)] += block
            else:
                gather[at(HALO - k)] = block
        for k, block in high_blocks:
            if k == 1:
                gather[at(HALO + OWN - 1)] += block
            else:
                gather[at(HALO + OWN - 2 + k)] = block

    place = lax.axis_index("row")
    odd = place & 1

    @pl.when(odd == 0)
    def _():
        take(unpack(other_ref, place > 0), unpack(pair_ref))

    @pl.when(odd == 1)
    def _():
        take(unpack(pair_ref), unpack(other_ref, place < lax.axis_size("row") - 1))

    for q in range(8):
        block = gather[pl.ds(16 + q, NB, stride=ROWS), :].T
        for g in range(4):
            coef[pl.ds((g * 8 + q) * 32, 32)] = block[g * 32:(g + 1) * 32]
    square = coef[pl.ds(0, SWEEPS, stride=33), :]
    all_tau = jnp.where(square > 0, 2.0 / jnp.where(square > 0, square, 1.0), 0.0)
    row = lax.broadcasted_iota(jnp.int32, (SWEEPS, NB), 0)
    for j in range(SWEEPS):
        mine = jnp.broadcast_to(all_tau[j:j + 1], (SWEEPS, NB))
        scaled = coef[pl.ds(j * 32, 32)] * jnp.where(row < j, all_tau, mine)
        if j >= WIDE - 1:
            coef[pl.ds(j * 32, 32)] = scaled
        count = 32 if j < WIDE else 16
        coef_half[pl.ds(j * 32, count)] = halves(scaled[:count], scaled[:count])

    for q in range(16):
        block = gather[pl.ds(q, NB, stride=ROWS), :].T
        parts = [block[g * 32:(g + 1) * 32] * all_tau for g in range(4)]
        for g in range(4):
            inner[pl.ds(g * 16 + q + 8 * EIG, 24, stride=64), :] = parts[g][8:]
        for g in range(2):
            inner_half[pl.ds(g * 16 + q, 16, stride=32), :] = halves(parts[g][:16], parts[g + 2][:16])

    copy_phase.wait()
    phases = [phase[j] for j in range(SWEEPS)]
    wide, half = shifted[:SWEEPS - WIDE], shifted[SWEEPS - WIDE:]
    lane = lax.broadcasted_iota(jnp.int32, (EIG // 2, NB), 1) & 63

    def keep_half(j, y):
        half[j][pl.ds(0, 32)] = jnp.where(lane == 0, 0.0, pltpu.roll(y, 1, 1))
        half[j][pl.ds(32, 32)] = jnp.where(lane == 63, 0.0, pltpu.roll(y, NB - 1, 1))

    for j in range(SWEEPS - 1, WIDE - 2, -1):
        total = inner[pl.ds(j * EIG, EIG)]
        for i in range(SWEEPS - 1, j, -1):
            same = coef[pl.ds(j * 32 + i, 1), :]
            next_to = coef[pl.ds(i * 32 + j, 1), :]
            start = pl.multiple_of(jnp.where(phases[j] < phases[i], 0, EIG), EIG)
            total = total - same * inner[pl.ds(i * EIG, EIG)] - next_to * wide[i - WIDE][pl.ds(start, EIG)]
        inner[pl.ds(j * EIG, EIG)] = total
        if j >= WIDE:
            wide[j - WIDE][pl.ds(0, EIG)] = pltpu.roll(total, 1, 1)
            wide[j - WIDE][pl.ds(EIG, EIG)] = pltpu.roll(total, NB - 1, 1)
        both = halves(total[:32], total[32:])
        inner_half[pl.ds(j * 32, 32)] = both
        keep_half(j, both)

    for j in range(WIDE - 2, -1, -1):
        total = inner_half[pl.ds(j * 32, 32)]
        for i in range(SWEEPS - 1, j, -1):
            same = coef_half[pl.ds(j * 32 + i, 1), :]
            next_to = coef_half[pl.ds(i * 32 + j, 1), :]
            start = pl.multiple_of(jnp.where(phases[j] < phases[i], 0, 32), 32)
            total = total - same * inner_half[pl.ds(i * 32, 32)] - next_to * half[i][pl.ds(start, 32)]
        inner_half[pl.ds(j * 32, 32)] = total
        if j > 0:
            keep_half(j, total)

    for t in range(8):
        parts = [inner_half[pl.ds(g * 16 + q * 8 + t, 32, stride=32), :] for q in range(2) for g in range(2)]
        block = jnp.concatenate(parts, axis=0).T
        for h in range(2):
            rows_t[pl.ds(h * 8 + t, 40, stride=16), :] = block[h * 64 + 8:h * 64 + 48]

    def copy_out(c):
        first = 0 if c == 0 else ENDS[c - 1]
        part = pl.ds(first * NB, (ENDS[c] - first) * NB)
        return pltpu.make_async_copy(result.at[:, part], out_ref.at[:, part], sems.at[c])

    group = lane_group(8)
    for a in range(OWN):
        cols = pl.ds(a * NB, NB)
        rows = pl.ds(a * 64, 64)
        of_head = rows_t[pl.ds((a + 8) * 16, 16)]
        of_tail = rows_t[pl.ds((a + 7) * 16, 16)]
        spread = [jnp.concatenate([jnp.where(group == q * 2 + g, y[h * 8:h * 8 + 8], 0.0)
                                   for h in range(2) for g in range(2) for q in range(2)], axis=0)
                  for y in (of_head, of_tail)]
        update = outer_products(jnp.concatenate(spread, axis=1), high_ref[rows], low_ref[rows])
        result[:, cols] = x_ref[:, cols] - update
        if a + 1 in ENDS:
            copy_out(ENDS.index(a + 1)).start()
    for c in range(len(ENDS)):
        copy_out(c).wait()


def call(kernel, name, out_shape, scratch, operands, space=pltpu.VMEM):
    vmem = pl.BlockSpec(memory_space=pltpu.VMEM)
    any_space = pl.BlockSpec(memory_space=pl.ANY)
    specs = [any_space if x.ndim == 1 else vmem for x in operands]
    return pl.pallas_call(
        kernel,
        out_shape=tuple(jax.ShapeDtypeStruct(*x) for x in out_shape),
        in_specs=specs,
        out_specs=(pl.BlockSpec(memory_space=space),) * len(out_shape),
        scratch_shapes=[pltpu.VMEM(x, F32) if isinstance(x, tuple) else x for x in scratch],
        compiler_params=pltpu.CompilerParams(vmem_limit_bytes=VMEM_LIMIT),
        name=name,
    )(*operands)


def back_transform(x, pieces, sweep_ranges):
    count = lax.axis_size("row")
    phase = sweep_ranges[:, 0] % NB
    message = ((17 * ROWS, NB), F32)
    own, to_pair, to_other, high, low, x = call(
        inner_kernel, "inner_products",
        [(((OWN + 1) * ROWS, NB), F32), message, message, ((OWN * 64, NB), BF16), ((OWN * 64, NB), BF16), ((EIG, OWN * NB), F32)],
        [(SWEEPS, OWN * NB)],
        [sweep_ranges, x, *pieces],
    )
    within = [(i, i ^ 1) for i in range(count)]
    across = [(i, (i + 1) % count) for i in range(1, count, 2)]
    across = across + [(t, s) for s, t in across]
    pair = lax.ppermute(to_pair, "row", within)
    other = lax.ppermute(to_other, "row", across)
    out, = call(
        apply_kernel, "apply_sweeps",
        [((EIG, OWN * NB), F32)],
        [(EIG, OWN * NB), pltpu.SemaphoreType.DMA((len(ENDS),)),
         pltpu.SMEM((SWEEPS,), jnp.int32), pltpu.SemaphoreType.DMA, (NB * ROWS, NB), (SWEEPS * 32, NB), (SWEEPS * 32, NB), (SWEEPS * EIG, NB), (SWEEPS * 32, NB), (40 * 16, NB)]
        + [(2 * EIG, NB)] * (SWEEPS - WIDE) + [(EIG, NB)] * SWEEPS,
        [phase, own, pair, other, x, high, low],
        pl.ANY,
    )
    return out


def sweep_pieces(reflectors):
    cols, count = lax.axis_size("col"), lax.axis_size("row")
    width = count // cols
    groups = [[g * width + q for q in range(width)] for g in range(cols)]
    mine = lax.all_to_all(
        reflectors.reshape(width, -1), "row", split_axis=0, concat_axis=0, tiled=True,
        axis_index_groups=groups,
    )
    pieces = []
    for k in range(cols):
        pairs = [
            (c * count + g * width + q, ((g - k) % cols) * count + c * width + q)
            for c in range(cols) for g in range(cols) for q in range(width)
        ]
        pieces.append(lax.ppermute(mine, ("col", "row"), pairs))
    return pieces


def per_device(eigenvectors, reflectors, sweep_ranges):
    pieces = sweep_pieces(reflectors)
    x = lax.all_to_all(eigenvectors.reshape(2, -1, OWN * NB), "row", split_axis=1, concat_axis=1, tiled=True)
    x = x.transpose(1, 0, 2)
    return back_transform(x, pieces, sweep_ranges)


def solution(mesh):
    placed = (P(("col", "row"), None), P("row", "col"), P())
    return jax.shard_map(
        per_device, mesh=mesh, in_specs=placed, out_specs=P("col", "row"), check_vma=False
    )
```
